128 devices in a mesh: dp: 8 (over y_hi, x), row: 4 (over z), col: 4 (over y_lo, core).
Axes of the slice: x: 4, y: 4 (y_hi: 2, y_lo: 2; y = y_hi * 2 + y_lo), z: 4, core: 2. Of those that a mesh axis runs over, the one named last changes fastest.
Arguments:
- tokens: bfloat16 [16384, 2048], P(('dp', 'row'), 'col'), may hold values from -6 to 6
- norm_gain: float32 [2048], P('col'), may hold values from 0.5 to 1.5
- norm_bias: float32 [2048], P('col'), may hold values from -1.5 to 1.5
- qkv_weight: bfloat16 [3, 2048, 2048], P(None, 'col', 'row'), may hold values from -0.125 to 0.125
- qkv_bias: bfloat16 [3, 2048], P(None, ('row', 'col')), may hold values from -1.5 to 1.5
- up_weight: bfloat16 [2048, 8192], P('col', 'row'), may hold values from -0.125 to 0.125
- up_bias: bfloat16 [8192], P(('row', 'col')), may hold values from -2.5 to 2.5
- out_weight: bfloat16 [2048, 2048], P('row', 'col'), may hold values from -0.5 to 0.5
- out_bias: bfloat16 [2048], P('col'), may hold values from -1.5 to 1.5
- down_weight: bfloat16 [8192, 2048], P('row', 'col'), may hold values from -0.0625 to 0.0625
- down_bias: bfloat16 [2048], P('col'), may hold values from -1.5 to 1.5
- cotangent: bfloat16 [16384, 2048], P(('dp', 'row'), 'col'), may hold values from -6 to 6
Outputs:
- layer_out: bfloat16 [16384, 2048], P(('dp', 'row'), 'col')
- tokens_grad: float32 [16384, 2048], P(('dp', 'row'), 'col')
- norm_gain_grad: float32 [2048], P('col')
- norm_bias_grad: float32 [2048], P('col')
- qkv_weight_grad: float32 [3, 2048, 2048], P(None, 'col', 'row')
- qkv_bias_grad: float32 [3, 2048], P(None, ('row', 'col'))
- up_weight_grad: float32 [2048, 8192], P('col', 'row')
- up_bias_grad: float32 [8192], P(('row', 'col'))
- out_weight_grad: float32 [2048, 2048], P('row', 'col')
- out_bias_grad: float32 [2048], P('col')
- down_weight_grad: float32 [8192, 2048], P('row', 'col')
- down_bias_grad: float32 [2048], P('col')
The draws below stay inside these ranges and needn't reach their ends.
All inputs are finite; a program needn't handle non-finite values.
Results may differ from the reference program's by a relative error of at most 0.014.
Values may be sent and summed in bfloat16 or wider, within the bound.
No kernel may reach another device: no remote copies, remote signals or barrier semaphores. Data moves between devices by JAX's collectives and lax.ppermute only.
A program may use at most 192 MiB of HBM per device.

```python
import math
import jax
import jax.numpy as jnp
from jax import lax

D = 2048
H = 32
HD = 64
ROT = 32
FF = 8192
SEQ_LEN = 1024
SEQS = 16
TOKENS = 16384


def block_scale(key, shape, shards, smallest, top_value):
    def one(dim, parts):
        heights = jax.random.uniform(jax.random.fold_in(jax.random.fold_in(key, 6), dim), (parts,), jnp.float32, smallest / len(shards), top_value / len(shards))
        return jnp.repeat(jnp.exp(heights), shape[dim] // parts).reshape((-1,) + (1,) * (len(shape) - dim - 1))

    gain = one(*shards[0])
    for cut in shards[1:]:
        gain = gain * one(*cut)
    return gain


def centred(stream_key, dims, spread, reach, split=(), kind=jnp.bfloat16):
    level = block_scale(stream_key, dims, split, -0.22, 0.18) if split else 1.0
    array = jax.random.normal(stream_key, dims, jnp.float32) * spread * level
    return jnp.minimum(jnp.maximum(array, -reach), reach).astype(kind)


def setup_inputs(seed: int = 0) -> dict:
    key_list = jax.random.split(jax.random.key(seed), 13)
    tokens = centred(key_list[0], (TOKENS, D), 1.0, 6.0, ((0, 32), (1, 4)))
    norm_gain = jnp.clip(1.0 + 0.1 * jax.random.normal(key_list[1], (D,), jnp.float32), 0.5, 1.5)
    norm_bias = centred(key_list[2], (D,), 0.3, 1.5, ((0, 4),), jnp.float32)
    qkv_weight = centred(key_list[3], (3, D, D), D ** -0.5, 0.125, ((1, 4), (2, 4)))
    qkv_bias = centred(key_list[4], (3, D), 0.3, 1.5, ((1, 16),))
    up_weight = centred(key_list[5], (D, FF), D ** -0.5, 0.125, ((0, 4), (1, 4)))
    up_bias = centred(key_list[6], (FF,), 0.5, 2.5, ((0, 16),))
    out_weight = centred(key_list[7], (D, D), (D // 16) ** -0.5, 0.5, ((0, 4), (1, 4)))
    out_bias = centred(key_list[8], (D,), 0.3, 1.5, ((0, 4),))
    down_weight = centred(key_list[9], (FF, D), FF ** -0.5, 0.0625, ((0, 4), (1, 4)))
    down_bias = centred(key_list[10], (D,), 0.3, 1.5, ((0, 4),))
    cotangent = centred(key_list[11], (TOKENS, D), 1.0, 6.0, ((0, 32), (1, 4)))
    return dict(tokens=tokens, norm_gain=norm_gain, norm_bias=norm_bias, qkv_weight=qkv_weight, qkv_bias=qkv_bias, up_weight=up_weight, up_bias=up_bias, out_weight=out_weight, out_bias=out_bias, down_weight=down_weight, down_bias=down_bias, cotangent=cotangent)


EPS = 1e-05
HIGHEST = lax.Precision.HIGHEST

@jax.custom_vjp
def low(v):
    return lax.optimization_barrier(v.astype(jnp.bfloat16)).astype(jnp.float32)

@jax.custom_vjp
def low_back(v):
    return v

def low_keep(v):
    return (low(v), None)

def low_pass(kept, grad):
    return (grad,)

def back_keep(v):
    return (v, None)

def back_low(kept, grad):
    return (low(grad),)
low.defvjp(low_keep, low_pass)
low_back.defvjp(back_keep, back_low)

def rotate(tensor, positions, direction_sign):
    half_rot = ROT // 2
    freq_index = jnp.arange(half_rot).astype(jnp.float32)
    inverse_freq = jnp.power(10000.0, -2.0 * freq_index / ROT)
    angles = positions.astype(jnp.float32)[:, None] * inverse_freq[None, :]
    cosine_table = jnp.cos(angles)[:, None, :]
    sine_table = direction_sign * jnp.sin(angles)[:, None, :]
    first_part = tensor[..., :half_rot]
    second_part = tensor[..., half_rot:ROT]
    remainder = tensor[..., ROT:]
    return jnp.concatenate([first_part * cosine_table - second_part * sine_table, second_part * cosine_table + first_part * sine_table, remainder], -1)

@jax.checkpoint
def sequence_attention(pieces):
    queries, keys_rot, values = pieces
    length = queries.shape[0]
    scores = jnp.einsum('qhd,khd->hqk', queries, keys_rot, precision=HIGHEST) * (1.0 / math.sqrt(HD))
    scores = low_back(scores)
    key_index = jnp.arange(length)
    allowed = key_index[None, :] <= key_index[:, None]
    scores = jnp.where(allowed[None], scores, -1e+30)
    weights_low = low(jax.nn.softmax(scores, axis=-1))
    return jnp.einsum('hqk,khd->qhd', weights_low, values, precision=HIGHEST)

def forward(inputs_f, norm_gain, norm_bias, qkv_weight, qkv_bias, up_weight, up_bias, out_weight, out_bias, down_weight, down_bias):
    group_rows = inputs_f.shape[0]
    center = lax.optimization_barrier(jnp.mean(inputs_f, -1, keepdims=True))
    variance = lax.optimization_barrier(jnp.mean((inputs_f - center) ** 2, -1, keepdims=True))
    normalized = (inputs_f - center) * lax.rsqrt(variance + EPS)
    normed = low(normalized * norm_gain + norm_bias)
    qkv_pre = jnp.einsum('td,wde->twe', normed, qkv_weight, precision=HIGHEST) + qkv_bias[None]
    up_pre = low_back(jnp.dot(normed, up_weight, precision=HIGHEST) + up_bias)
    positions = jnp.arange(group_rows) % SEQ_LEN
    heads_shape = (group_rows, H, HD)
    queries = low(rotate(low_back(qkv_pre[:, 0]).reshape(heads_shape), positions, 1.0))
    keys_rot = low(rotate(low_back(qkv_pre[:, 1]).reshape(heads_shape), positions, 1.0))
    values = low(low_back(qkv_pre[:, 2])).reshape(heads_shape)
    seq_count = group_rows // SEQ_LEN
    seq_shape = (seq_count, SEQ_LEN, H, HD)
    attended = lax.map(sequence_attention, (queries.reshape(seq_shape), keys_rot.reshape(seq_shape), values.reshape(seq_shape)))
    attended = low(low_back(attended.reshape(group_rows, D)))
    hidden = low(jax.nn.gelu(up_pre, approximate=True))
    attn_branch = jnp.dot(attended, out_weight, precision=HIGHEST) + out_bias
    ffn_branch = jnp.dot(hidden, down_weight, precision=HIGHEST) + down_bias
    return inputs_f + attn_branch + ffn_branch

def reference(tokens, norm_gain, norm_bias, qkv_weight, qkv_bias, up_weight, up_bias, out_weight, out_bias, down_weight, down_bias, cotangent):
    params = (norm_gain.astype(jnp.float32), norm_bias.astype(jnp.float32), qkv_weight.astype(jnp.float32), qkv_bias.astype(jnp.float32), up_weight.astype(jnp.float32), up_bias.astype(jnp.float32), out_weight.astype(jnp.float32), out_bias.astype(jnp.float32), down_weight.astype(jnp.float32), down_bias.astype(jnp.float32))
    per_group = math.gcd(SEQS, max(1, 4096 // SEQ_LEN))
    group_rows = per_group * SEQ_LEN
    group_count = TOKENS // group_rows
    input_groups = tokens.astype(jnp.float32).reshape(group_count, group_rows, D)
    cot_groups = cotangent.astype(jnp.float32).reshape(group_count, group_rows, D)

    def group_step(carry, pieces):
        input_group, cot_group = pieces
        result, pullback = jax.vjp(forward, input_group, *params)
        grads = pullback(cot_group)
        updated = tuple((total + piece for total, piece in zip(carry, grads[1:])))
        return (updated, (result, grads[0]))
    initial = tuple((jnp.zeros_like(param) for param in params))
    totals, (results, input_grads) = lax.scan(group_step, initial, (input_groups, cot_groups))
    return (results.reshape(TOKENS, D).astype(jnp.bfloat16), input_grads.reshape(TOKENS, D), totals[0], totals[1], totals[2], totals[3], totals[4], totals[5], totals[6], totals[7], totals[8], totals[9])
```

```python
import math

import jax
import jax.numpy as jnp
from jax import lax
from jax.experimental import pallas as pl
from jax.experimental.pallas import tpu as pltpu
from jax.sharding import PartitionSpec as P

D = 2048
HD = 64
ROT = 32
SEQ = 1024
EPS = 1e-05
BLK = 512
F32 = jnp.float32
BF16 = jnp.bfloat16
MIB = 1 << 20
GELU_C = math.sqrt(2.0 / math.pi)


def from_col(value, k):
    return lax.ppermute(value, "col", [(i, i ^ k) for i in range(4)])


def from_row(value, k):
    return lax.ppermute(value, "row", [((i + k) % 4, i) for i in range(4)])


def from_x(value, k):
    return lax.ppermute(value, "dp", [(i // 4 * 4 + (i + k) % 4, i) for i in range(8)])


def from_half(value):
    return lax.ppermute(value, "dp", [(i, (i + 4) % 8) for i in range(8)])


def after(value, *others):
    return lax.optimization_barrier((value, *others))[0]


def gather_group(own, start_after=None):
    across = from_col(own, 2)
    ring = own if start_after is None else after(own, *start_after)
    next_own, prev_own = from_row(ring, 1), from_row(ring, 3)
    next_across, prev_across = from_row(across, 1), from_row(across, 3)
    far_own, far_across = from_row(next_own, 1), from_row(prev_across, 3)
    even = [(own, across), (next_own, next_across), (far_own, far_across), (prev_own, prev_across)]
    return [[a, from_col(a, 1), b, from_col(b, 1)] for a, b in even]


def x_gather(value, x):
    nxt, prv = from_x(value, 1), from_x(value, 3)
    far = [from_x(nxt[0], 1), from_x(prv[1], 3)]
    done = []
    for k in range(2):
        ring = jnp.concatenate([value[k], nxt[k], far[k], prv[k]] * 2, 0)
        rows = value.shape[1]
        done.append(lax.dynamic_slice_in_dim(ring, ((4 - x) % 4) * rows, 4 * rows, 0))
    return done


def dot_nn(a, b):
    return jnp.dot(a, b, preferred_element_type=F32)


def dot_nt(a, b):
    return lax.dot_general(a, b, (((1,), (1,)), ((), ())), preferred_element_type=F32)


def dot_tn(a, b):
    return lax.dot_general(a, b, (((0,), (0,)), ((), ())), preferred_element_type=F32)


def turned(v, cosine, sine_up, sine_down):
    return v * cosine + pltpu.roll(v, 112, 1) * sine_up + pltpu.roll(v, 16, 1) * sine_down


VMEM = pl.BlockSpec(memory_space=pltpu.VMEM)
SMEM = pl.BlockSpec(memory_space=pltpu.SMEM)


def call(kernel, args, outs, flops, name, scratch=(), limit=24, smem=0, moved=6 * MIB):
    return pl.pallas_call(
        kernel,
        in_specs=[SMEM] * smem + [VMEM] * (len(args) - smem),
        out_specs=[VMEM] * len(outs),
        out_shape=[jax.ShapeDtypeStruct(s, t) for s, t in outs],
        scratch_shapes=scratch,
        compiler_params=pltpu.CompilerParams(vmem_limit_bytes=limit * MIB),
        cost_estimate=pl.CostEstimate(flops=flops, bytes_accessed=moved, transcendentals=0),
        name=name,
    )(*args)


STEP = 256


def front_kernel(j, r_ref, x0, x1, x2, x3, w0, w1, w2, w3, gain, shift, bias, cos_t, up_t, down_t,
                 normed_o, qkv_o, hidden_o, hidden_t, slope_o, *own_o):
    base = ((r_ref[0] + j) % 2) * BLK
    for i in range(BLK // STEP):
        rows = slice(i * STEP, (i + 1) * STEP)
        xs = [x[rows, :].astype(F32) for x in (x0, x1, x2, x3)]
        center = sum(jnp.sum(x, 1, keepdims=True) for x in xs) * (1.0 / D)
        xs = [x - center for x in xs]
        variance = sum(jnp.sum(x * x, 1, keepdims=True) for x in xs) * (1.0 / D)
        inv = lax.rsqrt(variance + EPS)
        acc = bias[...].astype(F32)
        for q, (x, w) in enumerate(zip(xs, (w0, w1, w2, w3))):
            cols = slice(q * BLK, (q + 1) * BLK)
            hat = x * inv
            if own_o and q == 0:
                own_o[0][rows, :] = hat
                own_o[1][rows, :] = inv
            normed = (hat * gain[:, cols] + shift[:, cols]).astype(BF16)
            normed_o[rows, cols] = normed
            acc = acc + dot_nn(normed, w[...])
        spot = pl.ds(pl.multiple_of(base + i * STEP, STEP), STEP)
        cosine, sine_up, sine_down = cos_t[spot, :], up_t[spot, :], down_t[spot, :]
        for k in range(2):
            qkv_o[rows, k * 128 : (k + 1) * 128] = turned(
                acc[:, k * 128 : (k + 1) * 128], cosine, sine_up, sine_down
            ).astype(BF16)
        qkv_o[rows, 256:384] = acc[:, 256:384].astype(BF16)
        u = acc[:, 384:]
        sq = u * u
        t = jnp.tanh(GELU_C * u * (1.0 + 0.044715 * sq))
        half = 0.5 * (1.0 + t)
        hidden = (u * half).astype(BF16)
        hidden_o[rows, :] = hidden
        hidden_t[:, rows] = hidden.T
        slope_o[rows, :] = half + (0.5 * GELU_C) * u * (1.0 - t * t) * (1.0 + (3 * 0.044715) * sq)


def front(j, r, xs, ws, gain, shift, bias, tables):
    outs = [((BLK, D), BF16), ((BLK, 384), BF16), ((BLK, BLK), BF16), ((BLK, BLK), BF16), ((BLK, BLK), F32)]
    if j == 0:
        outs += [((BLK, BLK), F32), ((BLK, 1), F32)]

    def kernel(*refs):
        front_kernel(j, *refs)

    return call(kernel, [r, *xs, *ws, gain, shift, bias, *tables], outs, 2 * BLK * D * 896, "front", smem=1)


def back_kernel(c0, c1, c2, c3, w0, w1, w2, w3, slope, att_o, up_o, up_t, up_sum, cot_sum):
    up_total = jnp.zeros((1, BLK), F32)
    for i in range(BLK // STEP):
        rows = slice(i * STEP, (i + 1) * STEP)
        acc = dot_nt(c0[rows, :], w0[...])
        for c, w in ((c1, w1), (c2, w2), (c3, w3)):
            acc = acc + dot_nt(c[rows, :], w[...])
        att_o[rows, :] = acc[:, :128].astype(BF16)
        up = (acc[:, 128:] * slope[rows, :]).astype(BF16)
        up_o[rows, :] = up
        up_t[:, rows] = up.T
        up_total = up_total + jnp.sum(up.astype(F32), 0, keepdims=True)
    up_sum[...] = up_total
    cot_sum[...] = jnp.sum(c0[...].astype(F32), 0, keepdims=True)


def back(cs, ws, slope):
    outs = [((BLK, 128), BF16), ((BLK, BLK), BF16), ((BLK, BLK), BF16), ((1, BLK), F32), ((1, BLK), F32)]
    return call(back_kernel, [*cs, *ws, slope], outs, 2 * BLK * D * 640, "back")


QB = 256


def attention_kernel(r_ref, qkv0, qkv1, qkv2, qkv3, grad0, grad1, grad2, grad3, cos_t, up_t, down_t,
                     att0, att1, att2, att3, qkvg0, qkvg1, qkvg2, qkvg3, att_t, qkvg_t, qkv_sum,
                     seq_in, seq_grad, att_s, qkvg_s, dk, dv):
    r = r_ref[0]
    qkvs, grads = (qkv0, qkv1, qkv2, qkv3), (grad0, grad1, grad2, grad3)
    atts, qkvgs = (att0, att1, att2, att3), (qkvg0, qkvg1, qkvg2, qkvg3)
    for j in range(4):
        spot = pl.ds(pl.multiple_of(((r + j) % 4) * BLK, BLK), BLK)
        seq_in[spot, :] = qkvs[j][...]
        seq_grad[spot, :] = grads[j][...]
    lane = lax.broadcasted_iota(jnp.int32, (1, 128), 1)
    heads = [lane < HD, lane >= HD]
    causal = lax.broadcasted_iota(jnp.int32, (QB, QB), 1) <= lax.broadcasted_iota(jnp.int32, (QB, QB), 0)
    scale = 1.0 / math.sqrt(HD)
    zero = jnp.zeros((), BF16)

    def sequence(s, carry):
        base = pl.multiple_of(s * SEQ, SEQ)
        dk[...] = jnp.zeros_like(dk)
        dv[...] = jnp.zeros_like(dv)
        for i in range(SEQ // QB):
            table = slice(i * QB, (i + 1) * QB)
            rows = pl.ds(pl.multiple_of(base + i * QB, QB), QB)
            length = (i + 1) * QB
            span = pl.ds(base, length)
            out = jnp.zeros((QB, 128), F32)
            dq = jnp.zeros((QB, 128), F32)
            q_all = seq_in[rows, 0:128] * jnp.asarray(scale, BF16)
            g_all = seq_grad[rows, :]
            keys = seq_in[span, 128:256]
            values = seq_in[span, 256:384]
            for head in heads:
                q = jnp.where(head, q_all, zero)
                g = jnp.where(head, g_all, zero)
                scores = dot_nt(q, keys)
                last = jnp.where(causal, scores[:, length - QB :], -1e30)
                scores = last if i == 0 else jnp.concatenate([scores[:, : length - QB], last], 1)
                peak = jnp.max(scores, 1, keepdims=True)
                powers = jnp.exp(scores - peak)
                probs = powers * (1.0 / jnp.sum(powers, 1, keepdims=True))
                low = probs.astype(BF16)
                out = out + dot_nn(low, jnp.where(head, values, zero))
                pg = dot_nt(g, values)
                prod = probs * pg
                score_grad = (prod - probs * jnp.sum(prod, 1, keepdims=True)).astype(BF16)
                dq = dq + dot_nn(score_grad, jnp.where(head, keys, zero))
                dk[:length, :] += dot_tn(score_grad, q)
                dv[:length, :] += dot_tn(low, g)
            att_s[rows, :] = out.astype(BF16)
            qkvg_s[rows, 0:128] = turned(
                dq * scale, cos_t[table, :], -up_t[table, :], -down_t[table, :]
            ).astype(BF16)
        whole = pl.ds(base, SEQ)
        qkvg_s[whole, 128:256] = turned(dk[...], cos_t[...], -up_t[...], -down_t[...]).astype(BF16)
        qkvg_s[whole, 256:384] = dv[...].astype(BF16)
        return carry

    lax.fori_loop(0, 2, sequence, 0)
    total = jnp.zeros((1, 384), F32)
    for j in range(4):
        spot = pl.ds(pl.multiple_of(((r + j) % 4) * BLK, BLK), BLK)
        att, qkvg = att_s[spot, :], qkvg_s[spot, :]
        atts[j][...] = att
        qkvgs[j][...] = qkvg
        att_t[:, j * BLK : (j + 1) * BLK] = att.T
        qkvg_t[:, j * BLK : (j + 1) * BLK] = qkvg.T
        total = total + jnp.sum(qkvg.astype(F32), 0, keepdims=True)
    qkv_sum[...] = total


def attention(r, qkvs, grads, tables):
    outs = (
        [((BLK, 128), BF16)] * 4
        + [((BLK, 384), BF16)] * 4
        + [((128, 2048), BF16), ((384, 2048), BF16), ((1, 384), F32)]
    )
    scratch = [
        pltpu.VMEM((2048, 384), BF16),
        pltpu.VMEM((2048, 128), BF16),
        pltpu.VMEM((2048, 128), BF16),
        pltpu.VMEM((2048, 384), BF16),
        pltpu.VMEM((SEQ, 128), F32),
        pltpu.VMEM((SEQ, 128), F32),
    ]
    out = call(attention_kernel, [r, *qkvs, *grads, *tables], outs, 12 << 30, "attention", scratch, 32, 1)
    return out[:4], out[4:8], out[8], out[9], out[10]


def chunks_out(x, held, outs):
    own, nxt, far_a, far_b, prv = outs
    own[...] = held[x]
    nxt[...] = held[(x + 1) % 4]
    prv[...] = held[(x + 3) % 4]
    far_a[...] = held[(x + 2) % 4, :, : D // 2]
    far_b[...] = held[(x + 2) % 4, :, D // 2 :]


def mlp_weights_kernel(x_ref, *refs):
    hid, upg, cots, normeds = refs[0:4], refs[4:8], refs[8:24], refs[24:28]
    outs, held = refs[28:33], refs[33]
    for q in range(4):
        cols = slice(q * BLK, (q + 1) * BLK)
        down = dot_nn(hid[0][...], cots[q][...])
        up = dot_nn(upg[0][...], normeds[0][:, cols])
        for j in range(1, 4):
            down = down + dot_nn(hid[j][...], cots[4 * j + q][...])
            up = up + dot_nn(upg[j][...], normeds[j][:, cols])
        for a in range(4):
            for h in range(2):
                rows = slice(a * 128 + h * 64, a * 128 + h * 64 + 64)
                held[a, h * 128 : h * 128 + 64, cols] = down[rows].astype(BF16)
                held[a, h * 128 + 64 : h * 128 + 128, cols] = up[rows].astype(BF16)
    chunks_out(x_ref[0], held, outs)


def att_weights_kernel(x_ref, att_t, qkvg_t, *refs):
    cots, normeds, outs, held = refs[0:16], refs[16:20], refs[20:25], refs[25]
    for q in range(4):
        cols = slice(q * BLK, (q + 1) * BLK)
        out = dot_nn(att_t[:, :BLK], cots[q][...])
        qkv = dot_nn(qkvg_t[:, :BLK], normeds[0][:, cols])
        for j in range(1, 4):
            span = slice(j * BLK, (j + 1) * BLK)
            out = out + dot_nn(att_t[:, span], cots[4 * j + q][...])
            qkv = qkv + dot_nn(qkvg_t[:, span], normeds[j][:, cols])
        for a in range(4):
            for h in range(2):
                at = a * 32 + h * 16
                held[a, h * 64 : h * 64 + 16, cols] = out[at : at + 16].astype(BF16)
                for w in range(3):
                    held[a, h * 64 + 16 * (w + 1) : h * 64 + 16 * (w + 2), cols] = qkv[
                        w * 128 + at : w * 128 + at + 16
                    ].astype(BF16)
    chunks_out(x_ref[0], held, outs)


def weights(kernel, x, args, rows, flops, name):
    outs = [((rows, D), BF16)] * 2 + [((rows, D // 2), BF16)] * 2 + [((rows, D), BF16)]
    return call(kernel, [x, *args], outs, flops, name, [pltpu.VMEM((4, rows, D), BF16)], 32, 1, 24 * MIB)


def odd_kernel(second, *refs):
    firsts, seconds, w1, w3, outs = refs[0:4], refs[4:8], refs[8], refs[9], refs[10:14]
    for j in range(4):
        for n, w in enumerate((w1, w3)):
            outs[j][:, n * BLK : (n + 1) * BLK] = second(firsts[j], seconds[j], w).astype(BF16)


def even_kernel(second, count, has_far, *refs):
    refs = list(refs)
    firsts, seconds, odds = refs[:count], refs[count : 2 * count], refs[2 * count : 3 * count]
    w0, w2 = refs[3 * count : 3 * count + 2]
    rest = refs[3 * count + 2 :]
    for j in range(count):
        for n, w in enumerate((w0, w2)):
            cols = slice(n * BLK, (n + 1) * BLK)
            total = second(firsts[j], seconds[j], w) + odds[j][:, cols].astype(F32)
            if has_far and n == j:
                total = total + rest[j][...].astype(F32)
            if has_far:
                rest[2 + j][:, cols] = total.astype(BF16)
            else:
                rest[n][...] = total.astype(rest[n].dtype)


def reduce_group(product, firsts, seconds, ws, flops, name):
    wide = ((BLK, 2 * BLK), BF16)

    def odd(*refs):
        odd_kernel(product, *refs)

    def plain(*refs):
        even_kernel(product, 1, False, *refs)

    def with_far(*refs):
        even_kernel(product, 2, True, *refs)

    odds = call(odd, [*firsts, *seconds, ws[1], ws[3]], [wide] * 4, flops // 2, name + "_odd")
    odds = [from_col(o, 1) for o in odds]
    low = [((BLK, BLK), BF16)] * 2
    far_a, far_b = call(
        plain, [firsts[2], seconds[2], odds[2], ws[0], ws[2]], low, flops // 8, name + "_far"
    )
    far_a, far_b = from_row(far_a, 3), from_row(far_b, 1)
    own_a, own_b = call(
        plain, [firsts[0], seconds[0], odds[0], ws[0], ws[2]], [((BLK, BLK), F32)] * 2, flops // 8, name + "_own"
    )
    nxt, prv = call(
        with_far,
        [firsts[1], firsts[3], seconds[1], seconds[3], odds[1], odds[3], ws[0], ws[2], far_a, far_b],
        [wide] * 2,
        flops // 4,
        name + "_near",
    )
    nxt, prv = from_row(nxt, 3), from_row(prv, 1)
    give = own_b + nxt[:, BLK:].astype(F32) + prv[:, BLK:].astype(F32)
    keep = own_a + nxt[:, :BLK].astype(F32) + prv[:, :BLK].astype(F32)
    return keep + from_col(give.astype(BF16), 2).astype(F32)


def sum_dp(chunks, half):
    own, nxt, far_a, far_b, prv = chunks
    far_a, far_b = from_x(far_a, 3), from_x(far_b, 1)
    nil = jnp.zeros_like(far_a)
    nxt = nxt.astype(F32) + jnp.concatenate([far_a, nil], 1).astype(F32)
    prv = prv.astype(F32) + jnp.concatenate([nil, far_b], 1).astype(F32)
    nxt, prv = from_x(nxt.astype(BF16), 3), from_x(prv.astype(BF16), 1)
    total = own.astype(F32) + nxt.astype(F32) + prv.astype(F32)
    rows = own.shape[0] // 2
    give = lax.dynamic_slice_in_dim(total, (1 - half) * rows, rows, 0).astype(BF16)
    keep = lax.dynamic_slice_in_dim(total, half * rows, rows, 0)
    mine = (keep + from_half(give).astype(F32)).astype(BF16)
    tiles = [mine[:, q * BLK : (q + 1) * BLK] for q in range(4)]
    tiles = jnp.stack([tiles[0]] + [from_col(tiles[q], q) for q in (1, 2, 3)])
    other = from_half(tiles)
    done = []
    for part, forward in ((tiles, 1), (other, 3)):
        near = {1: from_x(part, 1), 3: from_x(part, 3)}
        done.append([part, near[1], from_x(near[forward], forward), near[3]])
    return [[done[0][k], done[1][k]] for k in range(4)]


def unpack_mlp_kernel(s_ref, *refs):
    pieces, down_o, up_o, held = refs[:8], refs[8], refs[9], refs[10]
    for k in range(4):
        for e in range(2):
            at = ((s_ref[0] + k) % 4) * 128 + (s_ref[1] ^ e) * 64
            rows = pl.ds(pl.multiple_of(at, 64), 64)
            down_o[rows, :] = pieces[2 * k + e][0, :64, :].astype(F32)
            held[rows, :] = pieces[2 * k + e][0, 64:, :].astype(F32)
    up_o[...] = held[...].T


def unpack_att_kernel(s_ref, *refs):
    pieces, out_o, qkv_o, held = refs[:8], refs[8], refs[9], refs[10]
    for k in range(4):
        for e in range(2):
            at = ((s_ref[0] + k) % 4) * 32 + (s_ref[1] ^ e) * 16
            rows = pl.ds(pl.multiple_of(at, 16), 16)
            out_o[rows, :] = pieces[2 * k + e][0, :16, :].astype(F32)
            for w in range(3):
                held[w, rows, :] = pieces[2 * k + e][0, 16 * (w + 1) : 16 * (w + 2), :].astype(F32)
    for w in range(3):
        qkv_o[w] = held[w].T


def unpack(kernel, where, pieces, outs, scratch, name):
    rows = pieces[0][0].shape[1]
    return pl.pallas_call(
        kernel,
        grid_spec=pltpu.PrefetchScalarGridSpec(
            num_scalar_prefetch=1,
            grid=(4,),
            in_specs=[pl.BlockSpec((1, rows, BLK), lambda q, s: (q, 0, 0))] * 8,
            out_specs=[pl.BlockSpec(block, index) for block, index, _ in outs],
            scratch_shapes=[scratch],
        ),
        out_shape=[jax.ShapeDtypeStruct(shape, F32) for _, _, shape in outs],
        compiler_params=pltpu.CompilerParams(vmem_limit_bytes=24 * MIB),
        cost_estimate=pl.CostEstimate(flops=0, bytes_accessed=12 * MIB, transcendentals=0),
        name=name,
    )(where, *[p for pair in pieces for p in pair])


def rotation_tables():
    freq = jnp.power(10000.0, -2.0 * jnp.arange(ROT // 2).astype(F32) / ROT)
    angles = jnp.arange(SEQ).astype(F32)[:, None] * freq[None, :]
    cosine, sine = jnp.cos(angles), jnp.sin(angles)
    nil = jnp.zeros_like(sine)
    rest = jnp.zeros((SEQ, HD - ROT), F32)
    cos_t = jnp.concatenate([cosine, cosine, rest + 1.0] * 2, 1)
    up_t = jnp.concatenate([-sine, nil, rest] * 2, 1)
    down_t = jnp.concatenate([nil, sine, rest] * 2, 1)
    return cos_t, up_t, down_t


def shards(
    tokens,
    norm_gain,
    norm_bias,
    qkv_weight,
    qkv_bias,
    up_weight,
    up_bias,
    out_weight,
    out_bias,
    down_weight,
    down_bias,
    cotangent,
):
    r = lax.axis_index("row").astype(jnp.int32)
    c = lax.axis_index("col").astype(jnp.int32)
    g = lax.axis_index("dp").astype(jnp.int32)
    x, half = g % 4, g // 4
    r1, x1 = r.reshape(1), x.reshape(1)

    def piece_front(t, at, rows):
        heads = lax.dynamic_slice(qkv_weight, (0, at, t * 128), (3, rows, 128))
        hid = lax.dynamic_slice(up_weight, (at, t * BLK), (rows, BLK))
        return jnp.concatenate([heads[0], heads[1], heads[2], hid], 1)

    def piece_back(t):
        heads = lax.dynamic_slice_in_dim(out_weight, t * 128, 128, 0)
        hid = lax.dynamic_slice_in_dim(down_weight, t * BLK, BLK, 0)
        return jnp.concatenate([heads, hid], 0)

    def quarter_back(t):
        return lax.dynamic_slice_in_dim(piece_back(t), x * 160, 160, 0)

    norms = jnp.stack([norm_gain, norm_bias])
    norms = jnp.concatenate([norms] + [from_col(norms, k) for k in (1, 2, 3)], 1)
    gain, shift = norms[0:1], norms[1:2]
    bias = jnp.concatenate([qkv_bias[0], qkv_bias[1], qkv_bias[2], up_bias]).reshape(1, 896)
    tables = rotation_tables()

    xs = gather_group(tokens)
    quarter = jnp.stack([from_col(piece_front(c ^ k, x * 128, 128), k) for k in (2, 3)])
    wf2, wf3 = x_gather(quarter, x)
    wf = [piece_front(c, 0, BLK), from_col(piece_front(c ^ 1, 0, BLK), 1), wf2, wf3]
    late = after(cotangent, xs[0][2])
    ys = gather_group(late, (xs[1][2], xs[3][2]))
    quarter = jnp.stack([from_col(after(quarter_back(c ^ k), wf2), k) for k in (2, 3)])
    wb2, wb3 = x_gather(quarter, x)
    wb = [piece_back(c), from_col(piece_back(c ^ 1), 1), wb2, wb3]

    fronts = {j: front(j, r1, xs[j], wf, gain, shift, bias, tables) for j in (0, 1, 3, 2)}
    hat, inv = fronts[0][5:]
    normed, qkv, hidden, hidden_t, slope = [[fronts[j][n] for j in range(4)] for n in range(5)]
    backs = {j: back(ys[j], wb, slope[j]) for j in (0, 1, 3, 2)}
    att_grad, up_grad, up_grad_t, up_sums, cot_sums = [[backs[j][n] for j in range(4)] for n in range(5)]
    cots = [y for row in ys for y in row]

    first = weights(
        mlp_weights_kernel, x1, [*hidden_t, *up_grad_t, *cots, *normed], 256, 4 * 2048 * 2048 * BLK, "mlp_weights"
    )
    attended, qkv_grad, att_t, qkvg_t, qkv_sum = attention(r1, qkv, att_grad, tables)
    second = weights(
        att_weights_kernel, x1, [att_t, qkvg_t, *cots, *normed], 128, 2 * 2048 * 2048 * BLK, "att_weights"
    )

    first = sum_dp(first, half)
    second = sum_dp(second, half)

    normed_grad = reduce_group(
        lambda a, b, w: dot_nt(a[...], w[:, :384]) + dot_nt(b[...], w[:, 384:]),
        qkv_grad, up_grad, wf, 2 * 2048 * 2048 * 896, "norm_grad",
    )
    branch = reduce_group(
        lambda a, b, w: dot_nn(a[...], w[:128]) + dot_nn(b[...], w[128:]),
        attended, hidden, wb, 2 * 2048 * 2048 * 640, "layer",
    )
    layer_out = (
        tokens.astype(F32) + branch + out_bias.astype(F32) + down_bias.astype(F32)
    ).astype(BF16)

    biases = jnp.concatenate([qkv_sum, sum(up_sums), sum(cot_sums)], 1).reshape(11, 128)
    biases = biases + from_half(biases)
    biases = biases + from_x(biases, 1) + from_x(biases, 2) + from_x(biases, 3)
    biases = biases.reshape(-1)

    hat_grad = normed_grad * norm_gain
    sums = jnp.stack([jnp.sum(hat_grad, 1), jnp.sum(hat_grad * hat, 1)])
    sums = (sums + from_col(sums, 1) + from_col(sums, 2) + from_col(sums, 3)) / D
    tokens_grad = cotangent.astype(F32) + inv * (hat_grad - sums[0][:, None] - hat * sums[1][:, None])
    norm_grads = jnp.stack([jnp.sum(normed_grad * hat, 0), jnp.sum(normed_grad, 0)])
    norm_grads = norm_grads + from_row(norm_grads, 1) + from_row(norm_grads, 2) + from_row(norm_grads, 3)
    norm_grads = norm_grads + from_x(norm_grads, 1) + from_x(norm_grads, 2) + from_x(norm_grads, 3)
    norm_grads = norm_grads + from_half(norm_grads)

    where = jnp.stack([x, half, c])
    down_grad, up_wgrad = unpack(
        unpack_mlp_kernel, where, first,
        [
            ((BLK, BLK), lambda q, s: (s[2] ^ q, 0), (2048, BLK)),
            ((BLK, BLK), lambda q, s: (0, s[2] ^ q), (BLK, 2048)),
        ],
        pltpu.VMEM((BLK, BLK), F32), "unpack_mlp",
    )
    out_grad, qkv_wgrad = unpack(
        unpack_att_kernel, where, second,
        [
            ((128, BLK), lambda q, s: (s[2] ^ q, 0), (BLK, BLK)),
            ((3, BLK, 128), lambda q, s: (0, 0, s[2] ^ q), (3, BLK, BLK)),
        ],
        pltpu.VMEM((3, 128, BLK), F32), "unpack_att",
    )
    return (
        layer_out,
        tokens_grad,
        norm_grads[0],
        norm_grads[1],
        qkv_wgrad,
        biases[:384].reshape(3, 128),
        up_wgrad,
        biases[384:896],
        out_grad,
        biases[896:],
        down_grad,
        biases[896:],
    )


def solution(mesh):
    in_specs = (
        P(("dp", "row"), "col"),
        P("col"),
        P("col"),
        P(None, "col", "row"),
        P(None, ("row", "col")),
        P("col", "row"),
        P(("row", "col")),
        P("row", "col"),
        P("col"),
        P("row", "col"),
        P("col"),
        P(("dp", "row"), "col"),
    )
    out_specs = (
        P(("dp", "row"), "col"),
        P(("dp", "row"), "col"),
        P("col"),
        P("col"),
        P(None, "col", "row"),
        P(None, ("row", "col")),
        P("col", "row"),
        P(("row", "col")),
        P("row", "col"),
        P("col"),
        P("row", "col"),
        P("col"),
    )
    return jax.shard_map(shards, mesh=mesh, in_specs=in_specs, out_specs=out_specs, check_vma=False)
```

```python
import math

import jax
import jax.numpy as jnp
import numpy as np
from jax import lax
from jax.experimental import pallas as pl
from jax.experimental.pallas import tpu as pltpu
from jax.sharding import PartitionSpec as P

D = 2048
HD = 64
ROT = 32
SEQ = 1024
EPS = 1e-05
BLK = 512
F32 = jnp.float32
BF16 = jnp.bfloat16
MIB = 1 << 20
GELU_C = math.sqrt(2.0 / math.pi)


def from_col(value, k):
    return lax.ppermute(value, "col", [(i, i ^ k) for i in range(4)])


def from_row(value, k):
    return lax.ppermute(value, "row", [((i + k) % 4, i) for i in range(4)])


def from_x(value, k):
    return lax.ppermute(value, "dp", [(i // 4 * 4 + (i + k) % 4, i) for i in range(8)])


def from_half(value):
    return lax.ppermute(value, "dp", [(i, (i + 4) % 8) for i in range(8)])


def after(value, *others):
    return lax.optimization_barrier((value, *others))[0]


def dot_nn(a, b):
    return jnp.dot(a, b, preferred_element_type=F32)


def dot_nt(a, b):
    return lax.dot_general(a, b, (((1,), (1,)), ((), ())), preferred_element_type=F32)


def dot_tn(a, b):
    return lax.dot_general(a, b, (((0,), (0,)), ((), ())), preferred_element_type=F32)


def turned(v, cosine, sine_up, sine_down):
    return v * cosine + pltpu.roll(v, 112, 1) * sine_up + pltpu.roll(v, 16, 1) * sine_down


LIMITS = {'middle': 28, 'attention': 20}


def once(shape):
    return pl.BlockSpec(shape, lambda *_: (0,) * len(shape), pipeline_mode=pl.Buffered(1))


def call(kernel, name, grid, scalars, args, outs, scratch=(), aliases=None):
    return pl.pallas_call(
        kernel,
        grid_spec=pltpu.PrefetchScalarGridSpec(
            num_scalar_prefetch=1,
            grid=(grid,),
            in_specs=[spec for _, spec in args],
            out_specs=[spec for _, _, spec in outs],
            scratch_shapes=list(scratch),
        ),
        out_shape=[jax.ShapeDtypeStruct(shape, dtype) for shape, dtype, _ in outs],
        input_output_aliases=aliases or {},
        compiler_params=pltpu.CompilerParams(vmem_limit_bytes=next((v for k, v in LIMITS.items() if k in name), 56) * MIB),
        cost_estimate=pl.CostEstimate(flops=1000, bytes_accessed=1000, transcendentals=0),
        name=name,
    )(scalars, *[v for v, _ in args])


def full(array):
    return (array, once(array.shape))


def out_full(shape, dtype):
    return (shape, dtype, once(shape))


STEP = 256
PER = BLK // STEP


def packed(far, qkv, up, out, down):
    for w in range(3):
        far[w * 128 : (w + 1) * 128, :] = qkv(w)
    for n in range(4):
        far[384 + n * 128 : 512 + n * 128, :] = up(n)
        far[896 + n * 160 : 928 + n * 160, :] = out(n)
        far[928 + n * 160 : 1056 + n * 160, :] = down(n)


def lanes(t):
    return pl.ds(pl.multiple_of(t * 128, 128), 128)


def prep_near_kernel(s_ref, qkv, up, out, down, front, back, twin):
    c = s_ref[0]
    for w in range(3):
        front[:, w * 128 : (w + 1) * 128] = qkv[w, :, lanes(c)]
    front[:, 384:] = up[:, pl.ds(pl.multiple_of(c * BLK, BLK), BLK)]
    back[0:128, :] = out[lanes(c), :]
    back[128:, :] = down[pl.ds(pl.multiple_of(c * BLK, BLK), BLK), :]
    t = c ^ 1
    for k in range(4):
        feats = slice(k * 128, (k + 1) * 128)
        packed(
            twin.at[k],
            lambda w: qkv[w, feats, lanes(t)],
            lambda n: up[feats, lanes(t * 4 + n)],
            lambda n: out[pl.ds(pl.multiple_of(t * 128 + k * 32, 32), 32), n * 128 : (n + 1) * 128],
            lambda n: down[lanes(t * 4 + k), n * 128 : (n + 1) * 128],
        )


def prep_near(c, *raw):
    outs = [out_full((BLK, 896), BF16), out_full((640, BLK), BF16), out_full((4, 1536, 128), BF16)]
    return call(prep_near_kernel, "prep_near", 1, c, [full(w) for w in raw], outs)


def prep_far_kernel(s_ref, qkv, up, *refs):
    for n, k in enumerate((2, 3)):
        t = s_ref[0] ^ k
        out, down = refs[n], refs[2 + n]
        packed(
            refs[4 + n],
            lambda w: qkv[w, :, lanes(t)],
            lambda n: up[:, lanes(t * 4 + n)],
            lambda n: out[:, n * 128 : (n + 1) * 128],
            lambda n: down[:, n * 128 : (n + 1) * 128],
        )


def prep_far(c, x, qkv_weight, up_weight, out_weight, down_weight):
    args = [
        (qkv_weight, pl.BlockSpec((3, 128, BLK), lambda i, s: (0, s[1], 0))),
        (up_weight, pl.BlockSpec((128, 2048), lambda i, s: (s[1], 0))),
    ]
    args += [(out_weight, pl.BlockSpec((32, BLK), lambda i, s, k=k: ((s[0] ^ k) * 4 + s[1], 0))) for k in (2, 3)]
    args += [(down_weight, pl.BlockSpec((128, BLK), lambda i, s, k=k: ((s[0] ^ k) * 4 + s[1], 0))) for k in (2, 3)]
    return call(prep_far_kernel, "prep_far", 1, jnp.stack([c, x]), args, [out_full((1536, 128), BF16)] * 2)


def unpacked(part, place, wf, wb):
    feats = pl.ds(pl.multiple_of(place * 128, 128), 128)
    for n in range(7):
        wf[feats, n * 128 : (n + 1) * 128] = part[n * 128 : (n + 1) * 128, :]
    rows = pl.ds(pl.multiple_of(place * 32, 32), 32)
    wide = pl.ds(pl.multiple_of(128 + place * 128, 128), 128)
    for n in range(4):
        cols = slice(n * 128, (n + 1) * 128)
        wb[rows, cols] = part[896 + n * 160 : 928 + n * 160, :]
        wb[wide, cols] = part[928 + n * 160 : 1056 + n * 160, :]


def join_kernel(s_ref, own2, own3, nxt, prv, far2, far3, twin, wf1, wf2, wf3, wb1, wb2, wb3):
    x = s_ref[0]
    for k in range(4):
        unpacked(twin.at[k], k, wf1, wb1)
        unpacked((own2, nxt.at[0], far2, prv.at[0])[k], (x + k) % 4, wf2, wb2)
        unpacked((own3, nxt.at[1], far3, prv.at[1])[k], (x + k) % 4, wf3, wb3)


def join(x, parts):
    outs = [out_full((BLK, 896), BF16)] * 3 + [out_full((640, BLK), BF16)] * 3
    return call(join_kernel, "join", 1, x, [full(p) for p in parts], outs)


ORDER = (0, 1, 3, 2)
WIDTHS = ((D, BF16), (D, BF16), (384, BF16), (128, BF16), (BLK, BF16), (BLK, BF16))


def middle_kernel(extra, own, r_ref, *refs):
    step = pl.program_id(0)
    ps, rest = refs[:4], refs[4:]
    wf, wb = rest[0:4], rest[4:8]
    gain, shift, bias, cos_t, up_t, down_t = rest[8:14]
    rest = rest[14 + extra :]
    normed_o, cot_o, qkv_o, att_o, hidden_o, up_o, hidden_t, upg_t, up_sum, cot_sum = rest[:10]
    columns = [slice(q * BLK, (q + 1) * BLK) for q in range(4)]

    xs = [p[0].astype(F32) for p in ps]
    center = jnp.sum(xs[0] + xs[1] + xs[2] + xs[3], 1, keepdims=True) * (1.0 / D)
    xs = [x - center for x in xs]
    squares = xs[0] * xs[0] + xs[1] * xs[1] + xs[2] * xs[2] + xs[3] * xs[3]
    inv = lax.rsqrt(jnp.sum(squares, 1, keepdims=True) * (1.0 / D) + EPS)
    for q, cols in enumerate(columns):
        hat = xs[q] * inv
        if own and q == 0:
            rest[10][...] = hat
            rest[11][...] = inv
        normed_o[:, cols] = (hat * gain[:, cols] + shift[:, cols]).astype(BF16)
    acc = bias[...].astype(F32)
    grad = None
    for q, cols in enumerate(columns):
        acc = acc + dot_nn(normed_o[:, cols], wf[q][...])
        block = ps[q][1]
        cot_o[:, cols] = block
        term = dot_nt(block, wb[q][...])
        grad = term if grad is None else grad + term
    cosine, sine_up, sine_down = cos_t[...], up_t[...], down_t[...]
    for k in range(2):
        qkv_o[:, k * 128 : (k + 1) * 128] = turned(
            acc[:, k * 128 : (k + 1) * 128], cosine, sine_up, sine_down
        ).astype(BF16)
    qkv_o[:, 256:384] = acc[:, 256:384].astype(BF16)
    att_o[...] = grad[:, :128].astype(BF16)
    u = acc[:, 384:]
    sq = u * u
    t = jnp.tanh(GELU_C * u * (1.0 + 0.044715 * sq))
    half = 0.5 * (1.0 + t)
    hidden = (u * half).astype(BF16)
    hidden_o[...] = hidden
    hidden_t[...] = hidden.T
    slope = half + (0.5 * GELU_C) * u * (1.0 - t * t) * (1.0 + (3 * 0.044715) * sq)
    up = (grad[:, 128:] * slope).astype(BF16)
    up_o[...] = up
    upg_t[...] = up.T

    @pl.when(step == 0)
    def _():
        up_sum[...] = jnp.zeros_like(up_sum)
        cot_sum[...] = jnp.zeros_like(cot_sum)

    up_sum[...] += jnp.sum(up.astype(F32), 0, keepdims=True)
    cot_sum[...] += jnp.sum(ps[0][1].astype(F32), 0, keepdims=True)


def middle(r, n, pieces, shared, bufs=None):
    wf, wb, gain, shift, bias, tables = shared
    first, odd = n * PER, ORDER[n] % 2
    args = [(v, pl.BlockSpec((2, STEP, BLK), lambda i, r: (0, i, 0))) for v in pieces]
    args += [(v, pl.BlockSpec(memory_space=pltpu.VMEM)) for v in (*wf, *wb)]
    args += [full(v) for v in (gain, shift, bias)]
    args += [(t, pl.BlockSpec((STEP, 128), lambda i, r: ((r[0] + odd) % 2 * PER + i, 0))) for t in tables]
    aliases = {}
    if bufs is not None:
        aliases = {1 + len(args) + n: n for n in range(8)}
        args += [(v, pl.BlockSpec(memory_space=pl.ANY)) for v in bufs]
    outs = [((2048, w), t, pl.BlockSpec((STEP, w), lambda i, r: (first + i, 0))) for w, t in WIDTHS]
    outs += [((BLK, 2048), BF16, pl.BlockSpec((BLK, STEP), lambda i, r: (0, first + i)))] * 2
    outs += [out_full((1, BLK), F32)] * 2
    if bufs is None:
        outs += [((BLK, w), F32, pl.BlockSpec((STEP, w), lambda i, r: (i, 0))) for w in (BLK, 1)]

    def kernel(*refs):
        middle_kernel(len(aliases), bufs is None, *refs)

    return call(kernel, "middle", PER, r, args, outs, (), aliases)


QB = 256


def attention_kernel(r_ref, qkv, grad, cos_t, up_t, down_t, att_o, qkvg_o, att_t, qkvg_t, qkv_sum,
                     seq_in, seq_grad, att_s, qkvg_s, dk, dv):
    r = r_ref[0]

    def places():
        for n, j in enumerate(ORDER):
            yield slice(n * BLK, (n + 1) * BLK), pl.ds(pl.multiple_of(((r + j) % 4) * BLK, BLK), BLK)

    for here, spot in places():
        seq_in[spot, :] = qkv[here, :]
        seq_grad[spot, :] = grad[here, :]
    lane = lax.broadcasted_iota(jnp.int32, (1, 128), 1)
    heads = [lane < HD, lane >= HD]
    causal = lax.broadcasted_iota(jnp.int32, (QB, QB), 1) <= lax.broadcasted_iota(jnp.int32, (QB, QB), 0)
    scale = 1.0 / math.sqrt(HD)
    zero = jnp.zeros((), BF16)

    def sequence(s, carry):
        base = pl.multiple_of(s * SEQ, SEQ)
        dk[...] = jnp.zeros_like(dk)
        dv[...] = jnp.zeros_like(dv)
        for i in range(SEQ // QB):
            table = slice(i * QB, (i + 1) * QB)
            rows = pl.ds(pl.multiple_of(base + i * QB, QB), QB)
            length = (i + 1) * QB
            span = pl.ds(base, length)
            out = jnp.zeros((QB, 128), F32)
            dq = jnp.zeros((QB, 128), F32)
            q_all = seq_in[rows, 0:128] * jnp.asarray(scale, BF16)
            g_all = seq_grad[rows, :]
            keys = seq_in[span, 128:256]
            values = seq_in[span, 256:384]
            for head in heads:
                q = jnp.where(head, q_all, zero)
                g = jnp.where(head, g_all, zero)
                scores = dot_nt(q, keys)
                last = jnp.where(causal, scores[:, length - QB :], -1e30)
                scores = last if i == 0 else jnp.concatenate([scores[:, : length - QB], last], 1)
                peak = jnp.max(scores, 1, keepdims=True)
                powers = jnp.exp(scores - peak)
                probs = powers * (1.0 / jnp.sum(powers, 1, keepdims=True))
                low = probs.astype(BF16)
                out = out + dot_nn(low, jnp.where(head, values, zero))
                pg = dot_nt(g, values)
                prod = probs * pg
                score_grad = (prod - probs * jnp.sum(prod, 1, keepdims=True)).astype(BF16)
                dq = dq + dot_nn(score_grad, jnp.where(head, keys, zero))
                dk[:length, :] += dot_tn(score_grad, q)
                dv[:length, :] += dot_tn(low, g)
            att_s[rows, :] = out.astype(BF16)
            qkvg_s[rows, 0:128] = turned(
                dq * scale, cos_t[table, :], -up_t[table, :], -down_t[table, :]
            ).astype(BF16)
        whole = pl.ds(base, SEQ)
        qkvg_s[whole, 128:256] = turned(dk[...], cos_t[...], -up_t[...], -down_t[...]).astype(BF16)
        qkvg_s[whole, 256:384] = dv[...].astype(BF16)
        return carry

    lax.fori_loop(0, 2, sequence, 0)
    total = jnp.zeros((1, 384), F32)
    for here, spot in places():
        att, qkvg = att_s[spot, :], qkvg_s[spot, :]
        att_o[here, :] = att
        qkvg_o[here, :] = qkvg
        att_t[:, here] = att.T
        qkvg_t[:, here] = qkvg.T
        total = total + jnp.sum(qkvg.astype(F32), 0, keepdims=True)
    qkv_sum[...] = total


def attention(r, qkv, grad, tables):
    shapes = [((2048, 128), BF16), ((2048, 384), BF16), ((128, 2048), BF16), ((384, 2048), BF16), ((1, 384), F32)]
    scratch = [
        pltpu.VMEM((2048, 384), BF16),
        pltpu.VMEM((2048, 128), BF16),
        pltpu.VMEM((2048, 128), BF16),
        pltpu.VMEM((2048, 384), BF16),
        pltpu.VMEM((SEQ, 128), F32),
        pltpu.VMEM((SEQ, 128), F32),
    ]
    args = [full(v) for v in (qkv, grad, *tables)]
    return call(attention_kernel, "attention", 1, r, args, [out_full(*v) for v in shapes], scratch)


def chunks_out(x, held, outs):
    for k in range(4):
        outs[k][...] = held[(x + k) % 4]


def mlp_weights_kernel(x_ref, hidden_t, upg_t, cot, normed, *refs):
    outs, held = refs[:4], refs[4]
    down = dot_nn(hidden_t[...], cot[...])
    up = dot_nn(upg_t[...], normed[...])
    for a in range(4):
        for h in range(2):
            rows = slice(a * 128 + h * 64, a * 128 + h * 64 + 64)
            held[a, h * 128 : h * 128 + 64, :] = down[rows].astype(BF16)
            held[a, h * 128 + 64 : h * 128 + 128, :] = up[rows].astype(BF16)
    chunks_out(x_ref[0], held, outs)


def att_weights_kernel(x_ref, att_t, qkvg_t, cot, normed, *refs):
    outs, held = refs[:4], refs[4]
    out = dot_nn(att_t[...], cot[...])
    qkv = dot_nn(qkvg_t[...], normed[...])
    for a in range(4):
        for h in range(2):
            at = a * 32 + h * 16
            held[a, h * 64 : h * 64 + 16, :] = out[at : at + 16].astype(BF16)
            for w in range(3):
                held[a, h * 64 + 16 * (w + 1) : h * 64 + 16 * (w + 2), :] = qkv[
                    w * 128 + at : w * 128 + at + 16
                ].astype(BF16)
    chunks_out(x_ref[0], held, outs)


def weights(kernel, x, lefts, cot, normed, rows, name):
    column = lambda q, s: (0, q)
    args = [full(v) for v in lefts] + [(v, pl.BlockSpec((2048, BLK), column)) for v in (cot, normed)]
    outs = [((rows, D), BF16, pl.BlockSpec((rows, BLK), column))] * 4
    return call(kernel, name, 4, x, args, outs, [pltpu.VMEM((4, rows, BLK), BF16)])


def rows_of(width, first):
    return pl.BlockSpec((BLK, width), lambda i, s: (first + i, 0))


class GroupSum:
    def __init__(self, product, first, second, ws, name):
        self.product, self.first, self.second, self.ws, self.name = product, first, second, ws, name

    def run(self, kernel, name, start, blocks, ws, args, outs):
        first, second = self.first, self.second
        pair = [(first, rows_of(first.shape[1], start)), (second, rows_of(second.shape[1], start))]
        zero = jnp.zeros((1,), jnp.int32)
        return call(kernel, self.name + name, blocks, zero, pair + [full(w) for w in ws] + args, outs)

    def odd(self, *gate):
        if gate:
            self.first = after(self.first, *gate)

        def kernel(_, a, b, w1, w3, out):
            for n, w in enumerate((w1, w3)):
                out[:, n * BLK : (n + 1) * BLK] = self.product(a, b, w).astype(BF16)

        outs = [((2048, 2 * BLK), BF16, rows_of(2 * BLK, 0))]
        self.odds = self.run(kernel, "_odd", 0, 4, (self.ws[1], self.ws[3]), [], outs)[0]

    def swap(self, *gate):
        self.odds = from_col(after(self.odds, *gate) if gate else self.odds, 1)

    def even(self, name, start, more, outs, combine):
        def kernel(_, a, b, w0, w2, odds, *refs):
            for n, w in enumerate((w0, w2)):
                cols = slice(n * BLK, (n + 1) * BLK)
                combine(n, cols, self.product(a, b, w) + odds[:, cols].astype(F32), refs)

        args = [(self.odds, rows_of(2 * BLK, start))] + [(v, rows_of(v.shape[1], 0)) for v in more]
        return self.run(kernel, name, start, 1, (self.ws[0], self.ws[2]), args, outs)

    def far(self, *gate):
        if gate:
            self.odds = after(self.odds, *gate)

        def combine(n, cols, total, refs):
            refs[n][...] = total.astype(BF16)

        self.far_parts = self.even("_far", 3, [], [((BLK, BLK), BF16, rows_of(BLK, 0))] * 2, combine)

    def send_far(self, *gate):
        a, b = [after(v, *gate) for v in self.far_parts] if gate else self.far_parts
        self.far_sent = a, b
        self.far_parts = from_row(a, 3), from_row(b, 1)

    def near(self, *gate):
        if gate:
            self.odds = after(self.odds, *gate)

        def kernel(_, a, b, w0, w2, odds, *refs):
            for k in range(2):

                @pl.when(pl.program_id(0) == k)
                def _():
                    for n, w in enumerate((w0, w2)):
                        cols = slice(n * BLK, (n + 1) * BLK)
                        total = self.product(a, b, w) + odds[:, cols].astype(F32)
                        if n == k:
                            total = total + refs[k][...].astype(F32)
                        refs[2 + k][:, cols] = total.astype(BF16)

        args = [(self.odds, rows_of(2 * BLK, 1))] + [full(v) for v in self.far_parts]
        outs = [out_full((BLK, 2 * BLK), BF16)] * 2
        self.near_parts = self.run(kernel, "_near", 1, 2, (self.ws[0], self.ws[2]), args, outs)

    def send_near(self, *gate):
        a, b = [after(v, *gate) for v in self.near_parts] if gate else self.near_parts
        self.near_sent = a, b
        self.near_parts = from_row(a, 3), from_row(b, 1)

    def own(self, *gate):
        if gate:
            self.odds = after(self.odds, *gate)

        def combine(n, cols, total, refs):
            total = total + refs[0][:, cols].astype(F32) + refs[1][:, cols].astype(F32)
            refs[2 + n][...] = total.astype(refs[2 + n].dtype)

        outs = [((BLK, BLK), t, rows_of(BLK, 0)) for t in (F32, BF16)]
        self.keep, self.give = self.even("_own", 0, list(self.near_parts), outs, combine)

    def send_across(self, *gate):
        self.across = from_col(after(self.give, *gate) if gate else self.give, 2)

    def total(self):
        return self.keep + self.across.astype(F32)


def split_kernel(c_ref, *refs):
    parts, out = refs[:4], refs[4]
    rows = out.shape[1]
    for q in range(4):
        cols = slice(q * BLK, (q + 1) * BLK)
        total = sum(p[:, cols].astype(F32) for p in parts)
        for h in range(2):
            out[h * 4 + (c_ref[0] ^ q)] = total[h * rows : (h + 1) * rows].astype(BF16)


class WeightSum:
    def __init__(self, chunks):
        self.chunks = list(chunks)

    def send(self, steps, *gate):
        for k in steps:
            sent = after(self.chunks[k], *gate) if gate else self.chunks[k]
            self.chunks[k] = from_x(sent, 4 - k)

    def split(self, c, *gate):
        rows = self.chunks[0].shape[0] // 2
        own = after(self.chunks[0], *gate) if gate else self.chunks[0]
        args = [full(v) for v in (own, *self.chunks[1:])]
        self.parts = call(split_kernel, "split", 1, c, args, [out_full((8, rows, BLK), BF16)])[0]

    def exchange(self):
        groups = [[(h * 4 + x) * 4 + k for h in range(2) for k in range(4)] for x in range(4)]
        got = lax.all_to_all(self.parts, ("dp", "col"), 0, 0, tiled=True, axis_index_groups=groups)
        self.tiles = (got[:4].astype(F32) + got[4:].astype(F32)).astype(BF16)


class Gather:
    def __init__(self, tiles):
        self.tiles = tiles

    def first(self, *gate):
        t = after(self.tiles, *gate) if gate else self.tiles
        self.a = [self.tiles, from_x(t, 1), None, from_x(t, 3)]
        self.other = from_half(t)

    def second(self, *gate):
        t = after(self.other, *gate) if gate else self.other
        self.b = [self.other, from_x(t, 1), None, from_x(t, 3)]

    def third(self, *gate):
        a, b = self.a[1], self.b[3]
        if gate:
            a, b = after(a, *gate), after(b, *gate)
        self.a[2], self.b[2] = from_x(a, 1), from_x(b, 3)

    def pieces(self):
        return [p for pair in zip(self.a, self.b) for p in pair]


def unpack_kernel(s_ref, *refs):
    pieces, down_o, up_o, out_o, qkv_o, held_up, held = refs[:8], *refs[8:]
    for k in range(4):
        for e in range(2):
            piece = pieces[2 * k + e]
            place, half = (s_ref[0] + k) % 4, s_ref[1] ^ e
            rows = pl.ds(pl.multiple_of(place * 128 + half * 64, 64), 64)
            down_o[rows, :] = piece[0, :64, :].astype(F32)
            held_up[rows, :] = piece[0, 64:128, :].astype(F32)
            rows = pl.ds(pl.multiple_of(place * 32 + half * 16, 16), 16)
            out_o[rows, :] = piece[0, 128:144, :].astype(F32)
            for w in range(3):
                held[w, rows, :] = piece[0, 144 + 16 * w : 160 + 16 * w, :].astype(F32)
    up_o[...] = held_up[...].T
    for w in range(3):
        qkv_o[w] = held[w].T


def unpack(where, pieces):
    args = [(p, pl.BlockSpec((1, 192, BLK), lambda q, s: (q, 0, 0))) for p in pieces]
    outs = [
        ((2048, BLK), F32, pl.BlockSpec((BLK, BLK), lambda q, s: (q, 0))),
        ((BLK, 2048), F32, pl.BlockSpec((BLK, BLK), lambda q, s: (0, q))),
        ((BLK, BLK), F32, pl.BlockSpec((128, BLK), lambda q, s: (q, 0))),
        ((3, BLK, BLK), F32, pl.BlockSpec((3, BLK, 128), lambda q, s: (0, 0, q))),
    ]
    scratch = [pltpu.VMEM((BLK, BLK), F32), pltpu.VMEM((3, 128, BLK), F32)]
    return call(unpack_kernel, "unpack", 4, where, args, outs, scratch)


def rotation_tables():
    freq = np.power(np.float32(10000.0), np.float32(-2.0 / ROT) * np.arange(ROT // 2, dtype=np.float32))
    angles = (np.arange(SEQ, dtype=np.float32)[:, None] * freq[None, :]).astype(np.float64)
    cosine, sine = np.cos(angles), np.sin(angles)
    nil, rest = np.zeros_like(sine), np.zeros((SEQ, HD - ROT))
    tables = ([cosine, cosine, rest + 1.0], [-sine, nil, rest], [nil, sine, rest])
    return [jnp.asarray(np.concatenate(t * 2, 1).astype(np.float32)) for t in tables]


def shards(
    tokens,
    norm_gain,
    norm_bias,
    qkv_weight,
    qkv_bias,
    up_weight,
    up_bias,
    out_weight,
    out_bias,
    down_weight,
    down_bias,
    cotangent,
):
    r = lax.axis_index("row").astype(jnp.int32)
    c = lax.axis_index("col").astype(jnp.int32)
    g = lax.axis_index("dp").astype(jnp.int32)
    x, half = g % 4, g // 4
    r1, x1, c1 = r.reshape(1), x.reshape(1), c.reshape(1)

    own = jnp.stack([tokens, cotangent])
    raw = (qkv_weight, up_weight, out_weight, down_weight)
    far2, far3 = prep_far(c, x, *raw)
    nxt, prv = from_row(own, 1), from_row(own, 3)
    quarter2, quarter3 = from_col(far2, 2), from_col(far3, 3)
    norms = jnp.broadcast_to(jnp.stack([norm_gain, norm_bias])[None], (4, 2, BLK))
    norms = lax.all_to_all(norms, "col", 0, 0)
    own1 = from_col(own, 1)
    wf0, wb0, twin = prep_near(c1, after(raw[0], far2), *raw[1:])

    first = (nxt, prv, quarter2, quarter3, own1, twin, norms)
    far = jnp.stack([from_row(after(nxt[0], *first), 1), from_row(after(prv[1], *first), 3)])
    across = from_col(after(own, *first), 2)
    quarters = after(jnp.stack([quarter2, quarter3]), *first)
    quarters_nxt, quarters_prv = from_x(quarters, 1), from_x(quarters, 3)

    second = (far, across, quarters_nxt, quarters_prv)
    across1, twin = from_col(after(across, *second), 1), from_col(after(twin, *second), 1)
    ring, step = after(across, across1, twin), (across1, twin)
    nxt_across, prv_across = from_row(ring, 1), from_row(ring, 3)
    far_across = from_col(after(far, *step), 2)
    far2, far3 = from_x(after(quarters_nxt[0], *step), 1), from_x(after(quarters_prv[1], *step), 3)
    wf1, wf2, wf3, wb1, wb2, wb3 = join(
        x1, [quarter2, quarter3, quarters_nxt, quarters_prv, far2, far3, twin]
    )
    wf, wb = (wf0, wf1, wf2, wf3), (wb0, wb1, wb2, wb3)
    norms = [lax.dynamic_index_in_dim(norms, c ^ k, 0, False) for k in range(4)]
    norms = jnp.concatenate(norms, 1)
    gain, shift = norms[0:1], norms[1:2]
    bias = jnp.concatenate([qkv_bias[0], qkv_bias[1], qkv_bias[2], up_bias]).reshape(1, 896)
    tables = rotation_tables()
    shared = (wf, wb, gain, shift, bias, tables)
    done = middle(r1, 0, (own, own1, across, across1), shared)
    hat, inv = done[10:]
    up_sum, cot_sum = done[8], done[9]

    third = (nxt_across, prv_across, far_across, done[8])
    pieces = []
    for a, b in ((nxt, nxt_across), (prv, prv_across), (far, far_across)):
        pieces.append((a, from_col(after(a, *third), 1), b, from_col(after(b, *third), 1)))
    for n in range(3):
        done = middle(r1, n + 1, pieces[n], shared, done[:8])
        up_sum, cot_sum = up_sum + done[8], cot_sum + done[9]
    normed, cot, qkv, att_grad, hidden, up_grad, hidden_t, up_grad_t = done[:8]

    first = WeightSum(weights(mlp_weights_kernel, x1, [hidden_t, up_grad_t], cot, normed, 256, "mlp_weights"))
    own_chunk = first.chunks[0]
    first.send((1, 3))
    attended, qkv_grad, att_t, qkvg_t, qkv_sum = attention(r1, after(qkv, own_chunk), att_grad, tables)
    norm_sum = GroupSum(
        lambda a, b, w: dot_nt(a[...], w[:, :384]) + dot_nt(b[...], w[:, 384:]), qkv_grad, up_grad, wf, "norm_grad"
    )
    layer_sum = GroupSum(
        lambda a, b, w: dot_nn(a[...], w[:128]) + dot_nn(b[...], w[128:]), attended, hidden, wb, "layer"
    )

    norm_sum.odd()

    step = (first.chunks[1], first.chunks[3], norm_sum.odds)
    first.send((2,), *step)
    norm_sum.swap(*step)
    att_t = after(att_t, *step)
    second = WeightSum(weights(att_weights_kernel, x1, [att_t, qkvg_t], cot, normed, 128, "att_weights"))
    norm_sum.far(second.chunks[0])
    norm_sum.send_far()

    first.split(c1, *norm_sum.far_parts)
    first.exchange()
    second.send((1, 2, 3), first.parts)
    norm_sum.near(first.parts)
    norm_sum.send_near()
    layer_sum.odd(*norm_sum.near_sent)

    second.split(c1, layer_sum.odds, first.tiles, *norm_sum.near_parts)
    second.exchange()
    layer_sum.swap(second.parts)
    norm_sum.own(second.parts)
    layer_sum.far(second.tiles, norm_sum.give)

    gather = Gather(jnp.concatenate([first.tiles, second.tiles], 1))
    gather.first(norm_sum.give)
    layer_sum.send_far()
    layer_sum.near()
    step = (gather.a[1], gather.a[3], gather.other, *layer_sum.near_parts)
    gather.second(*step)
    layer_sum.send_near()
    norm_sum.send_across(*step)
    step = (gather.b[1], gather.b[3], norm_sum.across, *layer_sum.near_parts)
    gather.third(*step)
    layer_sum.own(*step)
    layer_sum.send_across()
    normed_grad = after(norm_sum.total(), *step)
    hat_grad = normed_grad * norm_gain
    sums = jnp.stack([jnp.sum(hat_grad, 1), jnp.sum(hat_grad * hat, 1)])
    sums = (sums + from_col(sums, 1) + from_col(sums, 2) + from_col(sums, 3)) / D
    norm_grads = jnp.stack([jnp.sum(normed_grad * hat, 0), jnp.sum(normed_grad, 0)])
    norm_grads = norm_grads + from_row(norm_grads, 1) + from_row(norm_grads, 2) + from_row(norm_grads, 3)
    tokens_grad = cotangent.astype(F32) + inv * (hat_grad - sums[0][:, None] - hat * sums[1][:, None])

    layer_out = (
        tokens.astype(F32) + layer_sum.total() + out_bias.astype(F32) + down_bias.astype(F32)
    ).astype(BF16)

    vectors = jnp.concatenate([qkv_sum, up_sum, cot_sum, norm_grads.reshape(1, 2 * BLK)], 1).reshape(19, 128)
    vectors = after(vectors, gather.a[2], gather.b[2])
    vectors = vectors + from_x(vectors, 1) + from_x(vectors, 2) + from_x(vectors, 3)
    vectors = (vectors + from_half(vectors)).reshape(-1)

    down_grad, up_wgrad, out_grad, qkv_wgrad = unpack(jnp.stack([x, half]), gather.pieces())
    out_bias_grad = vectors[896:1408]
    return (
        layer_out,
        tokens_grad,
        vectors[1408:1920],
        vectors[1920:],
        qkv_wgrad,
        vectors[:384].reshape(3, 128),
        up_wgrad,
        vectors[384:896],
        out_grad,
        out_bias_grad,
        down_grad,
        out_bias_grad,
    )


def solution(mesh):
    in_specs = (
        P(("dp", "row"), "col"),
        P("col"),
        P("col"),
        P(None, "col", "row"),
        P(None, ("row", "col")),
        P("col", "row"),
        P(("row", "col")),
        P("row", "col"),
        P("col"),
        P("row", "col"),
        P("col"),
        P(("dp", "row"), "col"),
    )
    out_specs = (
        P(("dp", "row"), "col"),
        P(("dp", "row"), "col"),
        P("col"),
        P("col"),
        P(None, "col", "row"),
        P(None, ("row", "col")),
        P("col", "row"),
        P(("row", "col")),
        P("row", "col"),
        P("col"),
        P("row", "col"),
        P("col"),
    )
    return jax.shard_map(shards, mesh=mesh, in_specs=in_specs, out_specs=out_specs, check_vma=False)
```

```python
import math
from types import SimpleNamespace

import jax
import jax.numpy as jnp
import numpy as np
from jax import lax
from jax.experimental import pallas as pl
from jax.experimental.pallas import tpu as pltpu
from jax.sharding import PartitionSpec as P

D = 2048
HD = 64
ROT = 32
SEQ = 1024
EPS = 1e-05
BLK = 512
F32 = jnp.float32
BF16 = jnp.bfloat16
MIB = 1 << 20
GELU_C = math.sqrt(2.0 / math.pi)


def from_col(value, k):
    return lax.ppermute(value, "col", [(i, i ^ k) for i in range(4)])


def from_row(value, k):
    return lax.ppermute(value, "row", [((i + k) % 4, i) for i in range(4)])


def from_x(value, k):
    return lax.ppermute(value, "dp", [(i // 4 * 4 + (i + k) % 4, i) for i in range(8)])


def from_half(value):
    return lax.ppermute(value, "dp", [(i, (i + 4) % 8) for i in range(8)])


def after(value, *others):
    return lax.optimization_barrier((value, *others))[0]


def dot_nn(a, b):
    return jnp.dot(a, b, preferred_element_type=F32)


def dot_nt(a, b):
    return lax.dot_general(a, b, (((1,), (1,)), ((), ())), preferred_element_type=F32)


def dot_tn(a, b):
    return lax.dot_general(a, b, (((0,), (0,)), ((), ())), preferred_element_type=F32)


def turned(v, cosine, sine_up, sine_down):
    return v * cosine + pltpu.roll(v, 112, 1) * sine_up + pltpu.roll(v, 16, 1) * sine_down


LIMITS = {}


def once(shape):
    return pl.BlockSpec(shape, lambda *_: (0,) * len(shape), pipeline_mode=pl.Buffered(1))


def call(kernel, name, grid, scalars, args, outs, scratch=(), aliases=None):
    return pl.pallas_call(
        kernel,
        grid_spec=pltpu.PrefetchScalarGridSpec(
            num_scalar_prefetch=1,
            grid=(grid,),
            in_specs=[spec for _, spec in args],
            out_specs=[spec for _, _, spec in outs],
            scratch_shapes=list(scratch),
        ),
        out_shape=[jax.ShapeDtypeStruct(shape, dtype) for shape, dtype, _ in outs],
        input_output_aliases=aliases or {},
        compiler_params=pltpu.CompilerParams(vmem_limit_bytes=next((v for k, v in LIMITS.items() if k in name), 52) * MIB),
        cost_estimate=pl.CostEstimate(flops=1000, bytes_accessed=1000, transcendentals=0),
        name=name,
    )(scalars, *[v for v, _ in args])


RESIDENT = pl.BlockSpec(memory_space=pltpu.VMEM)


def full(array):
    return (array, once(array.shape))


def out_full(shape, dtype):
    return (shape, dtype, once(shape))


STEP = 256
PER = BLK // STEP


def packed(far, qkv, up, out, down):
    for w in range(3):
        far[w * 128 : (w + 1) * 128, :] = qkv(w)
    for n in range(4):
        far[384 + n * 128 : 512 + n * 128, :] = up(n)
        far[896 + n * 160 : 928 + n * 160, :] = out(n)
        far[928 + n * 160 : 1056 + n * 160, :] = down(n)


def lanes(t):
    return pl.ds(pl.multiple_of(t * 128, 128), 128)


def prep_near_kernel(s_ref, qkv, up, out, down, front, back, twin):
    c = s_ref[0]
    for w in range(3):
        front[:, w * 128 : (w + 1) * 128] = qkv[w, :, lanes(c)]
    front[:, 384:] = up[:, pl.ds(pl.multiple_of(c * BLK, BLK), BLK)]
    back[0:128, :] = out[lanes(c), :]
    back[128:, :] = down[pl.ds(pl.multiple_of(c * BLK, BLK), BLK), :]
    t = c ^ 1
    for k in range(4):
        feats = slice(k * 128, (k + 1) * 128)
        packed(
            twin.at[k],
            lambda w: qkv[w, feats, lanes(t)],
            lambda n: up[feats, lanes(t * 4 + n)],
            lambda n: out[pl.ds(pl.multiple_of(t * 128 + k * 32, 32), 32), n * 128 : (n + 1) * 128],
            lambda n: down[lanes(t * 4 + k), n * 128 : (n + 1) * 128],
        )


def prep_near(c, *raw):
    outs = [((BLK, 896), BF16, RESIDENT), ((640, BLK), BF16, RESIDENT), out_full((4, 1536, 128), BF16)]
    return call(prep_near_kernel, "prep_near", 1, c, [full(w) for w in raw], outs)


def prep_far_kernel(s_ref, qkv, up, *refs):
    for n, k in enumerate((2, 3)):
        t = s_ref[0] ^ k
        out, down = refs[n], refs[2 + n]
        packed(
            refs[4 + n],
            lambda w: qkv[w, :, lanes(t)],
            lambda n: up[:, lanes(t * 4 + n)],
            lambda n: out[:, n * 128 : (n + 1) * 128],
            lambda n: down[:, n * 128 : (n + 1) * 128],
        )


def prep_far(c, x, qkv_weight, up_weight, out_weight, down_weight):
    args = [
        (qkv_weight, pl.BlockSpec((3, 128, BLK), lambda i, s: (0, s[1], 0))),
        (up_weight, pl.BlockSpec((128, 2048), lambda i, s: (s[1], 0))),
    ]
    args += [(out_weight, pl.BlockSpec((32, BLK), lambda i, s, k=k: ((s[0] ^ k) * 4 + s[1], 0))) for k in (2, 3)]
    args += [(down_weight, pl.BlockSpec((128, BLK), lambda i, s, k=k: ((s[0] ^ k) * 4 + s[1], 0))) for k in (2, 3)]
    return call(prep_far_kernel, "prep_far", 1, jnp.stack([c, x]), args, [out_full((1536, 128), BF16)] * 2)


def unpacked(part, place, wf, wb):
    feats = pl.ds(pl.multiple_of(place * 128, 128), 128)
    for n in range(7):
        wf[feats, n * 128 : (n + 1) * 128] = part[n * 128 : (n + 1) * 128, :]
    rows = pl.ds(pl.multiple_of(place * 32, 32), 32)
    wide = pl.ds(pl.multiple_of(128 + place * 128, 128), 128)
    for n in range(4):
        cols = slice(n * 128, (n + 1) * 128)
        wb[rows, cols] = part[896 + n * 160 : 928 + n * 160, :]
        wb[wide, cols] = part[928 + n * 160 : 1056 + n * 160, :]


def join_kernel(s_ref, own2, own3, nxt, prv, far2, far3, twin, wf1, wf2, wf3, wb1, wb2, wb3):
    x = s_ref[0]
    for k in range(4):
        unpacked(twin.at[k], k, wf1, wb1)
        unpacked((own2, nxt.at[0], far2, prv.at[0])[k], (x + k) % 4, wf2, wb2)
        unpacked((own3, nxt.at[1], far3, prv.at[1])[k], (x + k) % 4, wf3, wb3)


def join(x, parts):
    outs = [((BLK, 896), BF16, RESIDENT)] * 3 + [((640, BLK), BF16, RESIDENT)] * 3
    return call(join_kernel, "join", 1, x, [full(p) for p in parts], outs)


ORDER = (0, 1, 3, 2)
WIDTHS = ((D, BF16), (D, BF16), (384, BF16), (128, BF16), (BLK, BF16), (BLK, BF16))


def middle_kernel(extra, own, r_ref, *refs):
    step = pl.program_id(0)
    ps, rest = refs[:4], refs[4:]
    wf, wb = rest[0:4], rest[4:8]
    gain, shift, bias, cos_t, up_t, down_t = rest[8:14]
    rest = rest[14 + extra :]
    normed_o, cot_o, qkv_o, att_o, hidden_o, up_o, hidden_t, upg_t, up_sum, cot_sum = rest[:10]
    columns = [slice(q * BLK, (q + 1) * BLK) for q in range(4)]

    xs = [p[0].astype(F32) for p in ps]
    center = jnp.sum(xs[0] + xs[1] + xs[2] + xs[3], 1, keepdims=True) * (1.0 / D)
    xs = [x - center for x in xs]
    squares = xs[0] * xs[0] + xs[1] * xs[1] + xs[2] * xs[2] + xs[3] * xs[3]
    inv = lax.rsqrt(jnp.sum(squares, 1, keepdims=True) * (1.0 / D) + EPS)
    for q, cols in enumerate(columns):
        hat = xs[q] * inv
        if own and q == 0:
            rest[10][...] = hat
            rest[11][...] = inv
        normed_o[:, cols] = (hat * gain[:, cols] + shift[:, cols]).astype(BF16)
    acc = bias[...].astype(F32)
    grad = None
    for q, cols in enumerate(columns):
        acc = acc + dot_nn(normed_o[:, cols], wf[q][...])
        block = ps[q][1]
        cot_o[:, cols] = block
        term = dot_nt(block, wb[q][...])
        grad = term if grad is None else grad + term
    cosine, sine_up, sine_down = cos_t[...], up_t[...], down_t[...]
    for k in range(2):
        qkv_o[:, k * 128 : (k + 1) * 128] = turned(
            acc[:, k * 128 : (k + 1) * 128], cosine, sine_up, sine_down
        ).astype(BF16)
    qkv_o[:, 256:384] = acc[:, 256:384].astype(BF16)
    att_o[...] = grad[:, :128].astype(BF16)
    u = acc[:, 384:]
    sq = u * u
    t = jnp.tanh(GELU_C * u * (1.0 + 0.044715 * sq))
    half = 0.5 * (1.0 + t)
    hidden = (u * half).astype(BF16)
    hidden_o[...] = hidden
    hidden_t[...] = hidden.T
    slope = half + (0.5 * GELU_C) * u * (1.0 - t * t) * (1.0 + (3 * 0.044715) * sq)
    up = (grad[:, 128:] * slope).astype(BF16)
    up_o[...] = up
    upg_t[...] = up.T

    @pl.when(step == 0)
    def _():
        up_sum[...] = jnp.zeros_like(up_sum)
        cot_sum[...] = jnp.zeros_like(cot_sum)

    up_sum[...] += jnp.sum(up.astype(F32), 0, keepdims=True)
    cot_sum[...] += jnp.sum(ps[0][1].astype(F32), 0, keepdims=True)


def middle(r, n, pieces, shared, bufs=None):
    wf, wb, gain, shift, bias, tables = shared
    first, odd = n * PER, ORDER[n] % 2
    args = [(v, pl.BlockSpec((2, STEP, BLK), lambda i, r: (0, i, 0))) for v in pieces]
    args += [(v, RESIDENT) for v in (*wf, *wb)] + [full(v) for v in (gain, shift, bias)]
    args += [(t, pl.BlockSpec((STEP, 128), lambda i, r: ((r[0] + odd) % 2 * PER + i, 0))) for t in tables]
    aliases = {}
    if bufs is not None:
        aliases = {1 + len(args) + n: n for n in range(8)}
        args += [(v, pl.BlockSpec(memory_space=pl.ANY)) for v in bufs]
    outs = [((2048, w), t, pl.BlockSpec((STEP, w), lambda i, r: (first + i, 0))) for w, t in WIDTHS]
    outs += [((BLK, 2048), BF16, pl.BlockSpec((BLK, STEP), lambda i, r: (0, first + i)))] * 2
    outs += [out_full((1, BLK), F32)] * 2
    if bufs is None:
        outs += [((BLK, w), F32, pl.BlockSpec((STEP, w), lambda i, r: (i, 0))) for w in (BLK, 1)]

    def kernel(*refs):
        middle_kernel(len(aliases), bufs is None, *refs)

    return call(kernel, "middle", PER, r, args, outs, (), aliases)


QB = 256


def attention_kernel(r_ref, qkv, grad, cos_t, up_t, down_t, att_o, qkvg_o, att_t, qkvg_t, qkv_sum,
                     seq_in, seq_grad, att_s, qkvg_s, dk, dv):
    r = r_ref[0]

    def places():
        for n, j in enumerate(ORDER):
            yield slice(n * BLK, (n + 1) * BLK), pl.ds(pl.multiple_of(((r + j) % 4) * BLK, BLK), BLK)

    for here, spot in places():
        seq_in[spot, :] = qkv[here, :]
        seq_grad[spot, :] = grad[here, :]
    lane = lax.broadcasted_iota(jnp.int32, (1, 128), 1)
    heads = [lane < HD, lane >= HD]
    causal = lax.broadcasted_iota(jnp.int32, (QB, QB), 1) <= lax.broadcasted_iota(jnp.int32, (QB, QB), 0)
    scale = 1.0 / math.sqrt(HD)
    zero = jnp.zeros((), BF16)

    def sequence(s, carry):
        base = pl.multiple_of(s * SEQ, SEQ)
        dk[...] = jnp.zeros_like(dk)
        dv[...] = jnp.zeros_like(dv)
        for i in range(SEQ // QB):
            table = slice(i * QB, (i + 1) * QB)
            rows = pl.ds(pl.multiple_of(base + i * QB, QB), QB)
            length = (i + 1) * QB
            span = pl.ds(base, length)
            out = jnp.zeros((QB, 128), F32)
            dq = jnp.zeros((QB, 128), F32)
            q_all = seq_in[rows, 0:128] * jnp.asarray(scale, BF16)
            g_all = seq_grad[rows, :]
            keys = seq_in[span, 128:256]
            values = seq_in[span, 256:384]
            for head in heads:
                q = jnp.where(head, q_all, zero)
                g = jnp.where(head, g_all, zero)
                scores = dot_nt(q, keys)
                last = jnp.where(causal, scores[:, length - QB :], -1e30)
                scores = last if i == 0 else jnp.concatenate([scores[:, : length - QB], last], 1)
                peak = jnp.max(scores, 1, keepdims=True)
                powers = jnp.exp(scores - peak)
                probs = powers * (1.0 / jnp.sum(powers, 1, keepdims=True))
                low = probs.astype(BF16)
                out = out + dot_nn(low, jnp.where(head, values, zero))
                pg = dot_nt(g, values)
                prod = probs * pg
                score_grad = (prod - probs * jnp.sum(prod, 1, keepdims=True)).astype(BF16)
                dq = dq + dot_nn(score_grad, jnp.where(head, keys, zero))
                dk[:length, :] += dot_tn(score_grad, q)
                dv[:length, :] += dot_tn(low, g)
            att_s[rows, :] = out.astype(BF16)
            qkvg_s[rows, 0:128] = turned(
                dq * scale, cos_t[table, :], -up_t[table, :], -down_t[table, :]
            ).astype(BF16)
        whole = pl.ds(base, SEQ)
        qkvg_s[whole, 128:256] = turned(dk[...], cos_t[...], -up_t[...], -down_t[...]).astype(BF16)
        qkvg_s[whole, 256:384] = dv[...].astype(BF16)
        return carry

    lax.fori_loop(0, 2, sequence, 0)
    total = jnp.zeros((1, 384), F32)
    for here, spot in places():
        att, qkvg = att_s[spot, :], qkvg_s[spot, :]
        att_o[here, :] = att
        qkvg_o[here, :] = qkvg
        att_t[:, here] = att.T
        qkvg_t[:, here] = qkvg.T
        total = total + jnp.sum(qkvg.astype(F32), 0, keepdims=True)
    qkv_sum[...] = total


def attention(r, qkv, grad, tables):
    shapes = [((2048, 128), BF16), ((2048, 384), BF16), ((128, 2048), BF16), ((384, 2048), BF16), ((1, 384), F32)]
    scratch = [
        pltpu.VMEM((2048, 384), BF16),
        pltpu.VMEM((2048, 128), BF16),
        pltpu.VMEM((2048, 128), BF16),
        pltpu.VMEM((2048, 384), BF16),
        pltpu.VMEM((SEQ, 128), F32),
        pltpu.VMEM((SEQ, 128), F32),
    ]
    args = [full(v) for v in (qkv, grad, *tables)]
    return call(attention_kernel, "attention", 1, r, args, [out_full(*v) for v in shapes], scratch)


def chunks_out(x, held, outs):
    for k in range(4):
        outs[k][...] = held[(x + k) % 4]


def mlp_weights_kernel(x_ref, hidden_t, upg_t, cot, normed, *refs):
    outs, held = refs[:4], refs[4]
    down = dot_nn(hidden_t[...], cot[...])
    up = dot_nn(upg_t[...], normed[...])
    for a in range(4):
        for h in range(2):
            rows = slice(a * 128 + h * 64, a * 128 + h * 64 + 64)
            held[a, h * 128 : h * 128 + 64, :] = down[rows].astype(BF16)
            held[a, h * 128 + 64 : h * 128 + 128, :] = up[rows].astype(BF16)
    chunks_out(x_ref[0], held, outs)


def att_weights_kernel(x_ref, att_t, qkvg_t, cot, normed, *refs):
    outs, held = refs[:4], refs[4]
    held[0] = dot_nn(att_t[...], cot[...]).astype(BF16)
    qkv = dot_nn(qkvg_t[...], normed[...])
    for w in range(3):
        held[1 + w] = qkv[w * 128 : (w + 1) * 128].astype(BF16)
    chunks_out(x_ref[0], held, outs)


def weights(kernel, x, lefts, cot, normed, rows, name):
    column = lambda q, s: (0, q)
    args = [full(v) for v in lefts] + [(v, pl.BlockSpec((2048, BLK), column)) for v in (cot, normed)]
    outs = [((rows, D), BF16, pl.BlockSpec((rows, BLK), column))] * 4
    return call(kernel, name, 4, x, args, outs, [pltpu.VMEM((4, rows, BLK), BF16)])


def rows_of(width, first):
    return pl.BlockSpec((BLK, width), lambda i, s: (first + i, 0))


class GroupSum:
    def __init__(self, product, name):
        self.product, self.name = product, name

    def run(self, kernel, name, start, blocks, ws, args, outs, hold, scalars=None):
        first, second = hold(self.first), self.second
        pair = [(first, rows_of(first.shape[1], start)), (second, rows_of(second.shape[1], start))]
        if scalars is None:
            scalars = jnp.zeros((1,), jnp.int32)
        ws = [(self.ws[q], RESIDENT) for q in ws]
        return call(kernel, self.name + name, blocks, scalars, pair + ws + args, outs)

    def odd(self, hold):
        def kernel(_, a, b, w1, w3, out):
            for n, w in enumerate((w1, w3)):
                out[:, n * BLK : (n + 1) * BLK] = self.product(a, b, w).astype(BF16)

        outs = [((2048, 2 * BLK), BF16, rows_of(2 * BLK, 0))]
        self.odds = self.run(kernel, "_odd", 0, 4, (1, 3), [], outs, hold)[0]
        return [self.odds]

    def even(self, hold):
        def kernel(_, a, b, w0, w2, odds, *outs):
            totals = [self.product(a, b, w) for w in (w0, w2)]
            total = (jnp.concatenate(totals, 1) + odds[...].astype(F32)).astype(BF16)
            for k in range(3):

                @pl.when(pl.program_id(0) == k)
                def _():
                    outs[k][...] = total

        args = [(self.odds, rows_of(2 * BLK, 1))]
        outs = [out_full((BLK, 2 * BLK), BF16)] * 3
        self.parts = self.run(kernel, "_even", 1, 3, (0, 2), args, outs, hold)
        return self.parts

    def all_rows(self, r, hold):
        def kernel(_, a, b, w0, w2, odds, out):
            totals = [self.product(a, b, w) for w in (w0, w2)]
            out[0] = (jnp.concatenate(totals, 1) + odds[...].astype(F32)).astype(BF16)

        def place(i, s):
            return ((s[0] + jnp.where(i < 2, i, 5 - i)) % 4, 0, 0)

        args = [(self.odds, rows_of(2 * BLK, 0))]
        outs = [((4, BLK, 2 * BLK), BF16, pl.BlockSpec((1, BLK, 2 * BLK), place))]
        self.parts = self.run(kernel, "_rows", 0, 4, (0, 2), args, outs, hold, r)[0]
        return [self.parts]

    def own(self, hold):
        def kernel(_, a, b, w0, w2, odds, one, two, three, *outs):
            for n, w in enumerate((w0, w2)):
                cols = slice(n * BLK, (n + 1) * BLK)
                total = self.product(a, b, w)
                for v in (odds, one, two, three):
                    total = total + v[:, cols].astype(F32)
                outs[n][...] = total.astype(outs[n].dtype)

        args = [(v, rows_of(2 * BLK, 0)) for v in (self.odds, *self.got)]
        outs = [out_full((BLK, BLK), t) for t in (F32, BF16)]
        self.keep, self.give = self.run(kernel, "_own", 0, 1, (0, 2), args, outs, hold)
        return [self.give]

    def sum_rows(self, hold):
        got = hold(self.got)
        total = sum(got[k].astype(F32) for k in range(4))
        self.keep, self.give = total[:, :BLK], total[:, BLK:].astype(BF16)
        return [self.give]

    def move_swap(self, hold):
        self.odds = from_col(hold(self.odds), 1)
        return [self.odds]

    def move_rows(self, hold):
        self.got = [from_row(hold(v), k) for v, k in zip(self.parts, (3, 1, 2))]
        return self.got

    def exchange_rows(self, hold):
        self.got = lax.all_to_all(hold(self.parts), "row", 0, 0, tiled=True)
        return [self.got]

    def move_across(self, hold):
        self.across = from_col(hold(self.give), 2)
        return [self.across]

    def total(self):
        return self.keep + self.across.astype(F32)


def split_kernel(c_ref, *refs):
    parts, out = refs[:4], refs[4]
    rows = out.shape[1]
    for q in range(4):
        cols = slice(q * BLK, (q + 1) * BLK)
        total = sum(p[:, cols].astype(F32) for p in parts)
        for h in range(2):
            out[h * 4 + (c_ref[0] ^ q)] = total[h * rows : (h + 1) * rows].astype(BF16)


class WeightSum:
    def __init__(self, chunks):
        self.chunks = list(chunks)

    def send(self, steps, hold):
        for k in steps:
            self.chunks[k] = from_x(hold(self.chunks[k]), 4 - k)
        return [self.chunks[k] for k in steps]

    def split(self, c, hold):
        rows = self.chunks[0].shape[0] // 2
        args = [full(v) for v in (hold(self.chunks[0]), *self.chunks[1:])]
        self.parts = call(split_kernel, "split", 1, c, args, [out_full((8, rows, BLK), BF16)])[0]
        return [self.parts]

    def exchange(self, hold):
        groups = [[(h * 4 + x) * 4 + k for h in range(2) for k in range(4)] for x in range(4)]
        self.got = lax.all_to_all(hold(self.parts), ("dp", "col"), 0, 0, tiled=True, axis_index_groups=groups)
        return [self.got]

    def add(self, hold):
        got = hold(self.got)
        self.tiles = (got[:4].astype(F32) + got[4:].astype(F32)).astype(BF16)


class Gather:
    def __init__(self, tiles):
        self.tiles = tiles

    def first(self, hold):
        t = hold(self.tiles)
        self.a = [self.tiles, from_x(t, 1), None, from_x(t, 3)]
        return [self.a[1], self.a[3]]

    def other_half(self, hold):
        self.other = from_half(hold(self.tiles))
        return [self.other]

    def second(self, hold):
        t = hold(self.other)
        self.b = [self.other, from_x(t, 1), None, from_x(t, 3)]
        return [self.b[1], self.b[3]]

    def third(self, hold):
        self.a[2], self.b[2] = from_x(hold(self.a[1]), 1), from_x(hold(self.b[3]), 3)
        return [self.a[2], self.b[2]]

    def pieces(self):
        return [p for pair in zip(self.a, self.b) for p in pair]


def unpack_kernel(s_ref, *refs):
    pieces, down_o, up_o, out_o, qkv_o, held_up, held = refs[:8], *refs[8:]
    for k in range(4):
        for e in range(2):
            piece = pieces[2 * k + e]
            place, half = (s_ref[0] + k) % 4, s_ref[1] ^ e
            rows = pl.ds(pl.multiple_of(place * 128 + half * 64, 64), 64)
            down_o[rows, :] = piece[0, :64, :].astype(F32)
            held_up[rows, :] = piece[0, 64:128, :].astype(F32)
            held[place, pl.ds(pl.multiple_of(half * 64, 64), 64), :] = piece[0, 128:, :].astype(F32)
    up_o[...] = held_up[...].T
    out_o[...] = held[0]
    for w in range(3):
        qkv_o[w] = held[1 + w].T


def unpack(where, pieces):
    args = [(p, pl.BlockSpec((1, 192, BLK), lambda q, s: (q, 0, 0))) for p in pieces]
    outs = [
        ((2048, BLK), F32, pl.BlockSpec((BLK, BLK), lambda q, s: (q, 0))),
        ((BLK, 2048), F32, pl.BlockSpec((BLK, BLK), lambda q, s: (0, q))),
        ((BLK, BLK), F32, pl.BlockSpec((128, BLK), lambda q, s: (q, 0))),
        ((3, BLK, BLK), F32, pl.BlockSpec((3, BLK, 128), lambda q, s: (0, 0, q))),
    ]
    scratch = [pltpu.VMEM((BLK, BLK), F32), pltpu.VMEM((4, 128, BLK), F32)]
    return call(unpack_kernel, "unpack", 4, where, args, outs, scratch)


def rotation_tables():
    freq = np.power(np.float32(10000.0), np.float32(-2.0 / ROT) * np.arange(ROT // 2, dtype=np.float32))
    angles = (np.arange(SEQ, dtype=np.float32)[:, None] * freq[None, :]).astype(np.float64)
    cosine, sine = np.cos(angles), np.sin(angles)
    nil, rest = np.zeros_like(sine), np.zeros((SEQ, HD - ROT))
    tables = ([cosine, cosine, rest + 1.0], [-sine, nil, rest], [nil, sine, rest])
    return [jnp.asarray(np.concatenate(t * 2, 1).astype(np.float32)) for t in tables]


class Order:
    def __init__(self):
        self.before = []

    def hold(self):
        gate = tuple(self.before)
        return lambda value: after(value, *gate) if gate else value

    def do(self, step):
        self.before = list(step(self.hold()))

    def go(self, step):
        return list(step(self.hold()))

    def wait(self, arrivals):
        self.before = self.before + arrivals


def shards(
    tokens,
    norm_gain,
    norm_bias,
    qkv_weight,
    qkv_bias,
    up_weight,
    up_bias,
    out_weight,
    out_bias,
    down_weight,
    down_bias,
    cotangent,
):
    r = lax.axis_index("row").astype(jnp.int32)
    c = lax.axis_index("col").astype(jnp.int32)
    g = lax.axis_index("dp").astype(jnp.int32)
    x, half = g % 4, g // 4
    r1, x1, c1 = r.reshape(1), x.reshape(1), c.reshape(1)

    raw = (qkv_weight, up_weight, out_weight, down_weight)
    tables = rotation_tables()
    bias = jnp.concatenate([qkv_bias[0], qkv_bias[1], qkv_bias[2], up_bias]).reshape(1, 896)
    have = SimpleNamespace(own=jnp.stack([tokens, cotangent]), middle=None, sums_c=[])

    def send(name, source, move):
        def step(hold):
            setattr(have, name, move(hold(getattr(have, source))))
            return [getattr(have, name)]

        return step

    def twin(name):
        return send(name + "_twin", name, lambda v: from_col(v, 1))

    def over(name):
        return send(name + "_across", name, lambda v: from_col(v, 2))

    def own_rows(hold):
        own = hold(have.own)
        have.nxt, have.prv = from_row(own, 1), from_row(own, 3)
        return [have.nxt, have.prv]

    def far_prep(hold):
        have.packs = prep_far(c, x, hold(raw[0]), *raw[1:])
        return have.packs

    def near_prep(hold):
        have.wf0, have.wb0, have.pack = prep_near(c1, hold(raw[0]), *raw[1:])
        return [have.pack]

    def send_packs(hold):
        have.packs = [from_col(hold(v), k) for v, k in zip(have.packs, (2, 3))]
        return have.packs

    def send_norms(hold):
        norms = jnp.broadcast_to(hold(jnp.stack([norm_gain, norm_bias]))[None], (4, 2, BLK))
        have.norms = lax.all_to_all(norms, "col", 0, 0)
        return [have.norms]

    def send_far(hold):
        have.fars = [from_row(hold(have.nxt[0]), 1), from_row(hold(have.prv[1]), 3)]
        return have.fars

    def stack_far(hold):
        have.far = jnp.stack([hold(have.fars[0]), have.fars[1]])
        return [have.far]

    def stack_packs(hold):
        have.pair = jnp.stack([hold(have.packs[0]), have.packs[1]])
        return [have.pair]

    def send_pair(hold):
        pair = hold(have.pair)
        have.pairs = [from_x(pair, 1), from_x(pair, 3)]
        return have.pairs

    def slice_pairs(hold):
        nxt, prv = have.pairs
        have.pair_far = [hold(nxt[0]), prv[1]]
        return have.pair_far

    def send_pair_far(hold):
        a, b = have.pair_far
        have.pair_far = [from_x(hold(a), 1), from_x(hold(b), 3)]
        return have.pair_far

    def ring(hold):
        v = hold(have.across)
        have.nxt_across, have.prv_across = from_row(v, 1), from_row(v, 3)
        return [have.nxt_across, have.prv_across]

    def twins(names):
        parts = [twin(n) for n in names]
        return lambda hold: [v for p in parts for v in p(hold)]

    def join_packs(hold):
        parts = [hold(have.packs[0]), have.packs[1], *have.pairs, *have.pair_far, have.pack_twin]
        done = join(x1, parts)
        have.wf, have.wb = (have.wf0, *done[:3]), (have.wb0, *done[3:])
        return [done[0]]

    def middle_step(n):
        row = ("own", "nxt", "prv", "far")[n]
        across = ("across", "nxt_across", "prv_across", "far_across")[n]

        def step(hold):
            pieces = [getattr(have, k) for k in (row, row + "_twin", across, across + "_twin")]
            norms = [lax.dynamic_index_in_dim(have.norms, c ^ k, 0, False) for k in range(4)]
            norms = jnp.concatenate(norms, 1)
            shared = (have.wf, have.wb, norms[0:1], norms[1:2], bias, tables)
            done = middle(r1, n, [hold(pieces[0])] + pieces[1:], shared, have.middle)
            if n == 0:
                have.hat, have.inv = done[10:]
            have.middle = done[:8]
            have.sums_c = have.sums_c + [done[8:10]]
            return [done[8]]

        return step

    norm_sum = GroupSum(lambda a, b, w: dot_nt(a[...], w[:, :384]) + dot_nt(b[...], w[:, 384:]), "norm_grad")
    layer_sum = GroupSum(lambda a, b, w: dot_nn(a[...], w[:128]) + dot_nn(b[...], w[128:]), "layer")

    def mlp_weights(hold):
        normed, cot = have.middle[:2]
        lefts = [hold(have.middle[6]), have.middle[7]]
        have.first = WeightSum(weights(mlp_weights_kernel, x1, lefts, cot, normed, 256, "mlp_weights"))
        return have.first.chunks

    def attention_all(hold):
        qkv, att_grad, hidden, up_grad = have.middle[2:6]
        attended, qkv_grad, att_t, qkvg_t, qkv_sum = attention(r1, hold(qkv), att_grad, tables)
        norm_sum.first, norm_sum.second, norm_sum.ws = qkv_grad, up_grad, have.wf
        layer_sum.first, layer_sum.second, layer_sum.ws = attended, hidden, have.wb
        have.__dict__.update(att_t=att_t, qkvg_t=qkvg_t, qkv_sum=qkv_sum)
        return [qkv_sum]

    def att_weights(hold):
        normed, cot = have.middle[:2]
        lefts = [hold(have.att_t), have.qkvg_t]
        have.second = WeightSum(weights(att_weights_kernel, x1, lefts, cot, normed, 128, "att_weights"))
        return have.second.chunks

    def tiles(hold):
        first, second = have.first, have.second
        first.add(hold)
        second.add(hold)
        have.gather = Gather(jnp.concatenate([first.tiles, second.tiles], 1))
        return [have.gather.tiles]

    def normed_total(hold):
        normed_grad = hold(norm_sum.keep) + norm_sum.across.astype(F32)
        hat = have.hat
        up_sum, cot_sum = sum(v[0] for v in have.sums_c), sum(v[1] for v in have.sums_c)
        hat_grad = normed_grad * norm_gain
        have.hat_grad = hat_grad
        have.sums = jnp.stack([jnp.sum(hat_grad, 1), jnp.sum(hat_grad * hat, 1)])
        have.biases = jnp.concatenate([have.qkv_sum, up_sum, cot_sum], 1)
        have.norm_vectors = jnp.stack([jnp.sum(normed_grad * hat, 0), jnp.sum(normed_grad, 0)])
        return [have.sums, have.norm_vectors]

    def send_sums(hold):
        sums = hold(have.sums)
        have.sums_got = [from_col(sums, k) for k in (1, 2, 3)]
        return have.sums_got

    def vector_rows(hold):
        have.rows_got = [from_row(hold(have.norm_vectors), k) for k in (1, 2, 3)]
        return have.rows_got

    def vectors_x(hold):
        norms = have.norm_vectors + sum(have.rows_got)
        have.vectors = jnp.concatenate([have.biases, norms.reshape(1, 2 * BLK)], 1).reshape(19, 128)
        have.x_got = [from_x(hold(have.vectors), k) for k in (1, 2, 3)]
        return have.x_got

    def vectors_half(hold):
        have.vectors = have.vectors + sum(have.x_got)
        have.half_got = from_half(hold(have.vectors))
        return [have.half_got]

    def token_grads(hold):
        sums = (hold(have.sums) + sum(have.sums_got)) / D
        hat_grad, hat, inv = have.hat_grad, have.hat, have.inv
        have.tokens_grad = cotangent.astype(F32) + inv * (
            hat_grad - sums[0][:, None] - hat * sums[1][:, None]
        )
        return [have.tokens_grad]

    def unpack_all(hold):
        pieces = have.gather.pieces()
        have.weight_grads = unpack(jnp.stack([x, half]), [hold(pieces[0])] + pieces[1:])
        return have.weight_grads[2:3]

    def last_sum(hold):
        total = layer_sum.total() + out_bias.astype(F32) + down_bias.astype(F32)
        have.layer_out = (hold(tokens).astype(F32) + total).astype(BF16)
        return [have.layer_out]

    order = Order()
    own_rows_moved = order.go(own_rows)
    across_moved = order.go(send("across", "own", lambda v: from_col(v, 2)))
    order.do(far_prep)
    packs_moved = order.go(send_packs)
    own_twin_moved = order.go(twin("own"))
    norms_moved = order.go(send_norms)
    order.wait(packs_moved)
    order.do(stack_packs)
    pairs_moved = order.go(send_pair)
    order.wait(own_twin_moved)
    order.wait(norms_moved)
    order.wait(own_rows_moved)
    far_moved = order.go(send_far)
    order.do(near_prep)
    order.wait(far_moved)
    order.do(stack_far)
    across_twin_moved = order.go(twin("across"))
    order.wait(across_twin_moved)
    ring_moved = order.go(ring)
    order.go(over("far"))
    order.wait(across_moved)
    order.wait(pairs_moved)
    order.do(slice_pairs)
    order.go(send_pair_far)
    order.go(twin("pack"))
    order.do(join_packs)
    order.do(middle_step(0))
    order.go(twins(("nxt", "prv")))
    order.wait(ring_moved)
    far_twin_moved = order.go(twin("far"))
    ring_twins_moved = order.go(twins(("nxt_across", "prv_across")))
    far_across_twin_moved = order.go(twin("far_across"))
    order.wait(ring_twins_moved)
    order.do(middle_step(1))
    order.wait(far_twin_moved)
    order.do(middle_step(2))
    order.wait(far_across_twin_moved)
    order.do(middle_step(3))
    order.do(mlp_weights)
    first_near_moved = order.go(lambda hold: have.first.send((1, 3), hold))
    order.do(attention_all)
    order.do(norm_sum.odd)
    order.wait(first_near_moved)
    order.go(lambda hold: have.first.send((2,), hold))
    norm_swap_moved = order.go(norm_sum.move_swap)
    order.do(att_weights)
    second_far_moved = order.go(lambda hold: have.second.send((2,), hold))
    order.wait(norm_swap_moved)
    order.do(lambda hold: have.first.split(c1, hold))
    first_exchange_moved = order.go(lambda hold: have.first.exchange(hold))
    second_near_moved = order.go(lambda hold: have.second.send((1, 3), hold))
    order.do(norm_sum.even)
    norm_rows_moved = order.go(norm_sum.move_rows)
    order.do(layer_sum.odd)
    order.wait(first_exchange_moved)
    order.wait(second_far_moved)
    order.do(lambda hold: have.second.split(c1, hold))
    second_exchange_moved = order.go(lambda hold: have.second.exchange(hold))
    layer_swap_moved = order.go(layer_sum.move_swap)
    order.wait(second_near_moved)
    order.wait(second_exchange_moved)
    order.do(tiles)
    gather_half_moved = order.go(lambda hold: have.gather.other_half(hold))
    gather_a_moved = order.go(lambda hold: have.gather.first(hold))
    order.wait(layer_swap_moved)
    order.do(lambda hold: layer_sum.all_rows(r1, hold))
    layer_rows_moved = order.go(layer_sum.exchange_rows)
    order.wait(norm_rows_moved)
    order.do(norm_sum.own)
    norm_across_moved = order.go(norm_sum.move_across)
    order.wait(gather_half_moved)
    order.wait(gather_a_moved)
    gather_b_moved = order.go(lambda hold: have.gather.second(hold))
    order.wait(norm_across_moved)
    order.do(normed_total)
    sums_moved = order.go(send_sums)
    vector_rows_moved = order.go(vector_rows)
    order.wait(sums_moved)
    order.do(token_grads)
    order.wait(vector_rows_moved)
    order.wait(gather_b_moved)
    gather_far_moved = order.go(lambda hold: have.gather.third(hold))
    order.wait(layer_rows_moved)
    order.do(layer_sum.sum_rows)
    layer_across_moved = order.go(layer_sum.move_across)
    vectors_x_moved = order.go(vectors_x)
    order.wait(gather_far_moved)
    order.wait(vectors_x_moved)
    vectors_half_moved = order.go(vectors_half)
    order.do(unpack_all)
    order.wait(vectors_half_moved)
    order.wait(layer_across_moved)
    order.do(last_sum)
    down_grad, up_wgrad, out_grad, qkv_wgrad = have.weight_grads
    layer_out, tokens_grad = have.layer_out, have.tokens_grad
    vectors = (have.vectors + have.half_got).reshape(-1)
    biases, norm_grads = vectors[:1408], vectors[1408:]
    return (
        layer_out,
        tokens_grad,
        norm_grads[:BLK],
        norm_grads[BLK:],
        qkv_wgrad,
        biases[:384].reshape(3, 128),
        up_wgrad,
        biases[384:896],
        out_grad,
        biases[896:],
        down_grad,
        biases[896:],
    )


def solution(mesh):
    in_specs = (
        P(("dp", "row"), "col"),
        P("col"),
        P("col"),
        P(None, "col", "row"),
        P(None, ("row", "col")),
        P("col", "row"),
        P(("row", "col")),
        P("row", "col"),
        P("col"),
        P("row", "col"),
        P("col"),
        P(("dp", "row"), "col"),
    )
    out_specs = (
        P(("dp", "row"), "col"),
        P(("dp", "row"), "col"),
        P("col"),
        P("col"),
        P(None, "col", "row"),
        P(None, ("row", "col")),
        P("col", "row"),
        P(("row", "col")),
        P("row", "col"),
        P("col"),
        P("row", "col"),
        P("col"),
    )
    return jax.shard_map(shards, mesh=mesh, in_specs=in_specs, out_specs=out_specs, check_vma=False)
```

```python
import math
from types import SimpleNamespace

import jax
import jax.numpy as jnp
import numpy as np
from jax import lax
from jax.experimental import pallas as pl
from jax.experimental.pallas import tpu as pltpu
from jax.sharding import PartitionSpec as P

D = 2048
HD = 64
ROT = 32
SEQ = 1024
EPS = 1e-05
BLK = 512
F32 = jnp.float32
BF16 = jnp.bfloat16
MIB = 1 << 20
GELU_C = math.sqrt(2.0 / math.pi)


def from_col(value, k):
    return lax.ppermute(value, "col", [(i, i ^ k) for i in range(4)])


def from_row(value, k):
    return lax.ppermute(value, "row", [((i + k) % 4, i) for i in range(4)])


def from_x(value, k):
    return lax.ppermute(value, "dp", [(i // 4 * 4 + (i + k) % 4, i) for i in range(8)])


def from_half(value):
    return lax.ppermute(value, "dp", [(i, (i + 4) % 8) for i in range(8)])


def after(value, *others):
    return lax.optimization_barrier((value, *others))[0]


def dot_nn(a, b):
    return jnp.dot(a, b, preferred_element_type=F32)


def dot_nt(a, b):
    return lax.dot_general(a, b, (((1,), (1,)), ((), ())), preferred_element_type=F32)


def dot_tn(a, b):
    return lax.dot_general(a, b, (((0,), (0,)), ((), ())), preferred_element_type=F32)


def turned(v, cosine, sine_up, sine_down):
    return v * cosine + pltpu.roll(v, 112, 1) * sine_up + pltpu.roll(v, 16, 1) * sine_down


LIMITS = {}


def once(shape):
    return pl.BlockSpec(shape, lambda *_: (0,) * len(shape), pipeline_mode=pl.Buffered(1))


def call(kernel, name, grid, scalars, args, outs, scratch=(), aliases=None):
    return pl.pallas_call(
        kernel,
        grid_spec=pltpu.PrefetchScalarGridSpec(
            num_scalar_prefetch=1,
            grid=(grid,),
            in_specs=[spec for _, spec in args],
            out_specs=[spec for _, _, spec in outs],
            scratch_shapes=list(scratch),
        ),
        out_shape=[jax.ShapeDtypeStruct(shape, dtype) for shape, dtype, _ in outs],
        input_output_aliases=aliases or {},
        compiler_params=pltpu.CompilerParams(vmem_limit_bytes=next((v for k, v in LIMITS.items() if k in name), 52) * MIB),
        cost_estimate=pl.CostEstimate(flops=1000, bytes_accessed=1000, transcendentals=0),
        name=name,
    )(scalars, *[v for v, _ in args])


RESIDENT = pl.BlockSpec(memory_space=pltpu.VMEM)


def full(array):
    return (array, once(array.shape))


def out_full(shape, dtype):
    return (shape, dtype, once(shape))


STEP = 256
PER = BLK // STEP


def packed(far, qkv, up, out, down):
    for w in range(3):
        far[w * 128 : (w + 1) * 128, :] = qkv(w)
    for n in range(4):
        far[384 + n * 128 : 512 + n * 128, :] = up(n)
        far[896 + n * 160 : 928 + n * 160, :] = out(n)
        far[928 + n * 160 : 1056 + n * 160, :] = down(n)


def lanes(t):
    return pl.ds(pl.multiple_of(t * 128, 128), 128)


def prep_near_kernel(s_ref, qkv, up, out, down, front, back, twin):
    c = s_ref[0]
    for w in range(3):
        front[:, w * 128 : (w + 1) * 128] = qkv[w, :, lanes(c)]
    front[:, 384:] = up[:, pl.ds(pl.multiple_of(c * BLK, BLK), BLK)]
    back[0:128, :] = out[lanes(c), :]
    back[128:, :] = down[pl.ds(pl.multiple_of(c * BLK, BLK), BLK), :]
    t = c ^ 1
    for k in range(4):
        feats = slice(k * 128, (k + 1) * 128)
        packed(
            twin.at[k],
            lambda w: qkv[w, feats, lanes(t)],
            lambda n: up[feats, lanes(t * 4 + n)],
            lambda n: out[pl.ds(pl.multiple_of(t * 128 + k * 32, 32), 32), n * 128 : (n + 1) * 128],
            lambda n: down[lanes(t * 4 + k), n * 128 : (n + 1) * 128],
        )


def prep_near(c, *raw):
    outs = [((BLK, 896), BF16, RESIDENT), ((640, BLK), BF16, RESIDENT), out_full((4, 1536, 128), BF16)]
    return call(prep_near_kernel, "prep_near", 1, c, [full(w) for w in raw], outs)


def prep_far_kernel(s_ref, qkv, up, *refs):
    for n, k in enumerate((2, 3)):
        t = s_ref[0] ^ k
        out, down = refs[n], refs[2 + n]
        packed(
            refs[4 + n],
            lambda w: qkv[w, :, lanes(t)],
            lambda n: up[:, lanes(t * 4 + n)],
            lambda n: out[:, n * 128 : (n + 1) * 128],
            lambda n: down[:, n * 128 : (n + 1) * 128],
        )


def prep_far(c, x, qkv_weight, up_weight, out_weight, down_weight):
    args = [
        (qkv_weight, pl.BlockSpec((3, 128, BLK), lambda i, s: (0, s[1], 0))),
        (up_weight, pl.BlockSpec((128, 2048), lambda i, s: (s[1], 0))),
    ]
    args += [(out_weight, pl.BlockSpec((32, BLK), lambda i, s, k=k: ((s[0] ^ k) * 4 + s[1], 0))) for k in (2, 3)]
    args += [(down_weight, pl.BlockSpec((128, BLK), lambda i, s, k=k: ((s[0] ^ k) * 4 + s[1], 0))) for k in (2, 3)]
    return call(prep_far_kernel, "prep_far", 1, jnp.stack([c, x]), args, [out_full((1536, 128), BF16)] * 2)


def unpacked(part, place, wf, wb):
    feats = pl.ds(pl.multiple_of(place * 128, 128), 128)
    for n in range(7):
        wf[feats, n * 128 : (n + 1) * 128] = part[n * 128 : (n + 1) * 128, :]
    rows = pl.ds(pl.multiple_of(place * 32, 32), 32)
    wide = pl.ds(pl.multiple_of(128 + place * 128, 128), 128)
    for n in range(4):
        cols = slice(n * 128, (n + 1) * 128)
        wb[rows, cols] = part[896 + n * 160 : 928 + n * 160, :]
        wb[wide, cols] = part[928 + n * 160 : 1056 + n * 160, :]


def join_kernel(s_ref, own2, own3, nxt, prv, far2, far3, twin, wf1, wf2, wf3, wb1, wb2, wb3):
    x = s_ref[0]
    for k in range(4):
        unpacked(twin.at[k], k, wf1, wb1)
        unpacked((own2, nxt.at[0], far2, prv.at[0])[k], (x + k) % 4, wf2, wb2)
        unpacked((own3, nxt.at[1], far3, prv.at[1])[k], (x + k) % 4, wf3, wb3)


def join(x, parts):
    outs = [((BLK, 896), BF16, RESIDENT)] * 3 + [((640, BLK), BF16, RESIDENT)] * 3
    return call(join_kernel, "join", 1, x, [full(p) for p in parts], outs)


ORDER = (0, 1, 3, 2)
WIDTHS = ((D, BF16), (D, BF16), (384, BF16), (128, BF16), (BLK, BF16), (BLK, BF16))


def middle_kernel(extra, own, r_ref, *refs):
    step = pl.program_id(0)
    ps, rest = refs[:4], refs[4:]
    wf, wb = rest[0:4], rest[4:8]
    gain, shift, bias, cos_t, up_t, down_t = rest[8:14]
    rest = rest[14 + extra :]
    normed_o, cot_o, qkv_o, att_o, hidden_o, up_o, hidden_t, upg_t, up_sum, cot_sum = rest[:10]
    columns = [slice(q * BLK, (q + 1) * BLK) for q in range(4)]

    xs = [p[0].astype(F32) for p in ps]
    center = jnp.sum(xs[0] + xs[1] + xs[2] + xs[3], 1, keepdims=True) * (1.0 / D)
    xs = [x - center for x in xs]
    squares = xs[0] * xs[0] + xs[1] * xs[1] + xs[2] * xs[2] + xs[3] * xs[3]
    inv = lax.rsqrt(jnp.sum(squares, 1, keepdims=True) * (1.0 / D) + EPS)
    for q, cols in enumerate(columns):
        hat = xs[q] * inv
        if own and q == 0:
            rest[10][...] = hat
            rest[11][...] = inv
        normed_o[:, cols] = (hat * gain[:, cols] + shift[:, cols]).astype(BF16)
    acc = bias[...].astype(F32)
    grad = None
    for q, cols in enumerate(columns):
        acc = acc + dot_nn(normed_o[:, cols], wf[q][...])
        block = ps[q][1]
        cot_o[:, cols] = block
        term = dot_nt(block, wb[q][...])
        grad = term if grad is None else grad + term
    cosine, sine_up, sine_down = cos_t[...], up_t[...], down_t[...]
    for k in range(2):
        qkv_o[:, k * 128 : (k + 1) * 128] = turned(
            acc[:, k * 128 : (k + 1) * 128], cosine, sine_up, sine_down
        ).astype(BF16)
    qkv_o[:, 256:384] = acc[:, 256:384].astype(BF16)
    att_o[...] = grad[:, :128].astype(BF16)
    u = acc[:, 384:]
    sq = u * u
    t = jnp.tanh(GELU_C * u * (1.0 + 0.044715 * sq))
    half = 0.5 * (1.0 + t)
    hidden = (u * half).astype(BF16)
    hidden_o[...] = hidden
    hidden_t[...] = hidden.T
    slope = half + (0.5 * GELU_C) * u * (1.0 - t * t) * (1.0 + (3 * 0.044715) * sq)
    up = (grad[:, 128:] * slope).astype(BF16)
    up_o[...] = up
    upg_t[...] = up.T

    @pl.when(step == 0)
    def _():
        up_sum[...] = jnp.zeros_like(up_sum)
        cot_sum[...] = jnp.zeros_like(cot_sum)

    up_sum[...] += jnp.sum(up.astype(F32), 0, keepdims=True)
    cot_sum[...] += jnp.sum(ps[0][1].astype(F32), 0, keepdims=True)


def middle(r, n, pieces, shared, bufs=None):
    wf, wb, gain, shift, bias, tables = shared
    first, odd = n * PER, ORDER[n] % 2
    args = [(v, pl.BlockSpec((2, STEP, BLK), lambda i, r: (0, i, 0))) for v in pieces]
    args += [(v, RESIDENT) for v in (*wf, *wb)] + [full(v) for v in (gain, shift, bias)]
    args += [(t, pl.BlockSpec((STEP, 128), lambda i, r: ((r[0] + odd) % 2 * PER + i, 0))) for t in tables]
    aliases = {}
    if bufs is not None:
        aliases = {1 + len(args) + n: n for n in range(8)}
        args += [(v, pl.BlockSpec(memory_space=pl.ANY)) for v in bufs]
    outs = [((2048, w), t, pl.BlockSpec((STEP, w), lambda i, r: (first + i, 0))) for w, t in WIDTHS]
    outs += [((BLK, 2048), BF16, pl.BlockSpec((BLK, STEP), lambda i, r: (0, first + i)))] * 2
    outs += [out_full((1, BLK), F32)] * 2
    if bufs is None:
        outs += [((BLK, w), F32, pl.BlockSpec((STEP, w), lambda i, r: (i, 0))) for w in (BLK, 1)]

    def kernel(*refs):
        middle_kernel(len(aliases), bufs is None, *refs)

    return call(kernel, "middle", PER, r, args, outs, (), aliases)


QB = 256


def attention_kernel(r_ref, qkv, grad, cos_t, up_t, down_t, att_o, qkvg_o, att_t, qkvg_t, qkv_sum,
                     seq_in, seq_grad, att_s, qkvg_s, dk, dv):
    r = r_ref[0]

    def places():
        for n, j in enumerate(ORDER):
            yield slice(n * BLK, (n + 1) * BLK), pl.ds(pl.multiple_of(((r + j) % 4) * BLK, BLK), BLK)

    for here, spot in places():
        seq_in[spot, :] = qkv[here, :]
        seq_grad[spot, :] = grad[here, :]
    lane = lax.broadcasted_iota(jnp.int32, (1, 128), 1)
    heads = [lane < HD, lane >= HD]
    causal = lax.broadcasted_iota(jnp.int32, (QB, QB), 1) <= lax.broadcasted_iota(jnp.int32, (QB, QB), 0)
    scale = 1.0 / math.sqrt(HD)
    zero = jnp.zeros((), BF16)

    def sequence(s, carry):
        base = pl.multiple_of(s * SEQ, SEQ)
        dk[...] = jnp.zeros_like(dk)
        dv[...] = jnp.zeros_like(dv)
        for i in range(SEQ // QB):
            table = slice(i * QB, (i + 1) * QB)
            rows = pl.ds(pl.multiple_of(base + i * QB, QB), QB)
            length = (i + 1) * QB
            span = pl.ds(base, length)
            out = jnp.zeros((QB, 128), F32)
            dq = jnp.zeros((QB, 128), F32)
            q_all = seq_in[rows, 0:128] * jnp.asarray(scale, BF16)
            g_all = seq_grad[rows, :]
            keys = seq_in[span, 128:256]
            values = seq_in[span, 256:384]
            for head in heads:
                q = jnp.where(head, q_all, zero)
                g = jnp.where(head, g_all, zero)
                scores = dot_nt(q, keys)
                last = jnp.where(causal, scores[:, length - QB :], -1e30)
                scores = last if i == 0 else jnp.concatenate([scores[:, : length - QB], last], 1)
                peak = jnp.max(scores, 1, keepdims=True)
                powers = jnp.exp(scores - peak)
                probs = powers * (1.0 / jnp.sum(powers, 1, keepdims=True))
                low = probs.astype(BF16)
                out = out + dot_nn(low, jnp.where(head, values, zero))
                pg = dot_nt(g, values)
                prod = probs * pg
                score_grad = (prod - probs * jnp.sum(prod, 1, keepdims=True)).astype(BF16)
                dq = dq + dot_nn(score_grad, jnp.where(head, keys, zero))
                dk[:length, :] += dot_tn(score_grad, q)
                dv[:length, :] += dot_tn(low, g)
            att_s[rows, :] = out.astype(BF16)
            qkvg_s[rows, 0:128] = turned(
                dq * scale, cos_t[table, :], -up_t[table, :], -down_t[table, :]
            ).astype(BF16)
        whole = pl.ds(base, SEQ)
        qkvg_s[whole, 128:256] = turned(dk[...], cos_t[...], -up_t[...], -down_t[...]).astype(BF16)
        qkvg_s[whole, 256:384] = dv[...].astype(BF16)
        return carry

    lax.fori_loop(0, 2, sequence, 0)
    total = jnp.zeros((1, 384), F32)
    for here, spot in places():
        att, qkvg = att_s[spot, :], qkvg_s[spot, :]
        att_o[here, :] = att
        qkvg_o[here, :] = qkvg
        att_t[:, here] = att.T
        qkvg_t[:, here] = qkvg.T
        total = total + jnp.sum(qkvg.astype(F32), 0, keepdims=True)
    qkv_sum[...] = total


def attention(r, qkv, grad, tables):
    shapes = [((2048, 128), BF16), ((2048, 384), BF16), ((128, 2048), BF16), ((384, 2048), BF16), ((1, 384), F32)]
    scratch = [
        pltpu.VMEM((2048, 384), BF16),
        pltpu.VMEM((2048, 128), BF16),
        pltpu.VMEM((2048, 128), BF16),
        pltpu.VMEM((2048, 384), BF16),
        pltpu.VMEM((SEQ, 128), F32),
        pltpu.VMEM((SEQ, 128), F32),
    ]
    args = [full(v) for v in (qkv, grad, *tables)]
    return call(attention_kernel, "attention", 1, r, args, [out_full(*v) for v in shapes], scratch)


def chunks_out(x, held, outs):
    for k in range(4):
        outs[k][...] = held[(x + k) % 4]


def mlp_weights_kernel(x_ref, hidden_t, upg_t, cot, normed, *refs):
    outs, held = refs[:4], refs[4]
    down = dot_nn(hidden_t[...], cot[...])
    up = dot_nn(upg_t[...], normed[...])
    for a in range(4):
        for h in range(2):
            rows = slice(a * 128 + h * 64, a * 128 + h * 64 + 64)
            held[a, h * 128 : h * 128 + 64, :] = down[rows].astype(BF16)
            held[a, h * 128 + 64 : h * 128 + 128, :] = up[rows].astype(BF16)
    chunks_out(x_ref[0], held, outs)


def att_weights_kernel(x_ref, att_t, qkvg_t, cot, normed, *refs):
    outs, held = refs[:4], refs[4]
    held[0] = dot_nn(att_t[...], cot[...]).astype(BF16)
    qkv = dot_nn(qkvg_t[...], normed[...])
    for w in range(3):
        held[1 + w] = qkv[w * 128 : (w + 1) * 128].astype(BF16)
    chunks_out(x_ref[0], held, outs)


def weights(kernel, x, lefts, cot, normed, rows, name):
    column = lambda q, s: (0, q)
    args = [full(v) for v in lefts] + [(v, pl.BlockSpec((2048, BLK), column)) for v in (cot, normed)]
    outs = [((rows, D), BF16, pl.BlockSpec((rows, BLK), column))] * 4
    return call(kernel, name, 4, x, args, outs, [pltpu.VMEM((4, rows, BLK), BF16)])


def rows_of(width, first):
    return pl.BlockSpec((BLK, width), lambda i, s: (first + i, 0))


class GroupSum:
    def __init__(self, product, name):
        self.product, self.name = product, name

    def run(self, kernel, name, start, blocks, ws, args, outs, hold, scalars=None):
        first, second = hold(self.first), self.second
        pair = [(first, rows_of(first.shape[1], start)), (second, rows_of(second.shape[1], start))]
        if scalars is None:
            scalars = jnp.zeros((1,), jnp.int32)
        ws = [(self.ws[q], RESIDENT) for q in ws]
        return call(kernel, self.name + name, blocks, scalars, pair + ws + args, outs)

    def odd(self, hold):
        def kernel(_, a, b, w1, w3, out):
            for n, w in enumerate((w1, w3)):
                out[:, n * BLK : (n + 1) * BLK] = self.product(a, b, w).astype(BF16)

        outs = [((2048, 2 * BLK), BF16, rows_of(2 * BLK, 0))]
        self.odds = self.run(kernel, "_odd", 0, 4, (1, 3), [], outs, hold)[0]
        return [self.odds]

    def even(self, hold):
        def kernel(_, a, b, w0, w2, odds, *outs):
            totals = [self.product(a, b, w) for w in (w0, w2)]
            total = (jnp.concatenate(totals, 1) + odds[...].astype(F32)).astype(BF16)
            for k in range(3):

                @pl.when(pl.program_id(0) == k)
                def _():
                    outs[k][...] = total

        args = [(self.odds, rows_of(2 * BLK, 1))]
        outs = [out_full((BLK, 2 * BLK), BF16)] * 3
        self.parts = self.run(kernel, "_even", 1, 3, (0, 2), args, outs, hold)
        return self.parts

    def all_rows(self, r, hold):
        def kernel(_, a, b, w0, w2, odds, out):
            totals = [self.product(a, b, w) for w in (w0, w2)]
            out[0] = (jnp.concatenate(totals, 1) + odds[...].astype(F32)).astype(BF16)

        def place(i, s):
            return ((s[0] + jnp.where(i < 2, i, 5 - i)) % 4, 0, 0)

        args = [(self.odds, rows_of(2 * BLK, 0))]
        outs = [((4, BLK, 2 * BLK), BF16, pl.BlockSpec((1, BLK, 2 * BLK), place))]
        self.parts = self.run(kernel, "_rows", 0, 4, (0, 2), args, outs, hold, r)[0]
        return [self.parts]

    def own(self, hold):
        def kernel(_, a, b, w0, w2, odds, one, two, three, *outs):
            for n, w in enumerate((w0, w2)):
                cols = slice(n * BLK, (n + 1) * BLK)
                total = self.product(a, b, w)
                for v in (odds, one, two, three):
                    total = total + v[:, cols].astype(F32)
                outs[n][...] = total.astype(outs[n].dtype)

        args = [(v, rows_of(2 * BLK, 0)) for v in (self.odds, *self.got)]
        outs = [out_full((BLK, BLK), t) for t in (F32, BF16)]
        self.keep, self.give = self.run(kernel, "_own", 0, 1, (0, 2), args, outs, hold)
        return [self.give]

    def sum_rows(self, hold):
        got = hold(self.got)
        total = sum(got[k].astype(F32) for k in range(4))
        self.keep, self.give = total[:, :BLK], total[:, BLK:].astype(BF16)
        return [self.give]

    def move_swap(self, hold):
        self.odds = from_col(hold(self.odds), 1)
        return [self.odds]

    def move_rows(self, hold):
        self.got = [from_row(hold(v), k) for v, k in zip(self.parts, (3, 1, 2))]
        return self.got

    def exchange_rows(self, hold):
        self.got = lax.all_to_all(hold(self.parts), "row", 0, 0, tiled=True)
        return [self.got]

    def move_across(self, hold):
        self.across = from_col(hold(self.give), 2)
        return [self.across]

    def total(self):
        return self.keep + self.across.astype(F32)


def split_kernel(c_ref, *refs):
    parts, out = refs[:4], refs[4]
    rows = out.shape[1]
    for q in range(4):
        cols = slice(q * BLK, (q + 1) * BLK)
        total = sum(p[:, cols].astype(F32) for p in parts)
        for h in range(2):
            out[h * 4 + (c_ref[0] ^ q)] = total[h * rows : (h + 1) * rows].astype(BF16)


class WeightSum:
    def __init__(self, chunks):
        self.chunks = list(chunks)

    def send(self, steps, hold):
        for k in steps:
            self.chunks[k] = from_x(hold(self.chunks[k]), 4 - k)
        return [self.chunks[k] for k in steps]

    def split(self, c, hold):
        rows = self.chunks[0].shape[0] // 2
        args = [full(v) for v in (hold(self.chunks[0]), *self.chunks[1:])]
        self.parts = call(split_kernel, "split", 1, c, args, [out_full((8, rows, BLK), BF16)])[0]
        return [self.parts]

    def exchange(self, hold):
        groups = [[(h * 4 + x) * 4 + k for h in range(2) for k in range(4)] for x in range(4)]
        self.got = lax.all_to_all(hold(self.parts), ("dp", "col"), 0, 0, tiled=True, axis_index_groups=groups)
        return [self.got]

    def add(self, hold):
        got = hold(self.got)
        self.tiles = (got[:4].astype(F32) + got[4:].astype(F32)).astype(BF16)


class Gather:
    def __init__(self, tiles):
        self.tiles = tiles

    def first(self, hold):
        t = hold(self.tiles)
        self.a = [self.tiles, from_x(t, 1), None, from_x(t, 3)]
        return [self.a[1], self.a[3]]

    def other_half(self, hold):
        self.other = from_half(hold(self.tiles))
        return [self.other]

    def second(self, hold):
        t = hold(self.other)
        self.b = [self.other, from_x(t, 1), None, from_x(t, 3)]
        return [self.b[1], self.b[3]]

    def third(self, hold):
        self.a[2], self.b[2] = from_x(hold(self.a[1]), 1), from_x(hold(self.b[3]), 3)
        return [self.a[2], self.b[2]]

    def pieces(self):
        return [p for pair in zip(self.a, self.b) for p in pair]


def unpack_kernel(s_ref, *refs):
    pieces, down_o, up_o, out_o, qkv_o, held_up, held = refs[:8], *refs[8:]
    for k in range(4):
        for e in range(2):
            piece = pieces[2 * k + e]
            place, half = (s_ref[0] + k) % 4, s_ref[1] ^ e
            rows = pl.ds(pl.multiple_of(place * 128 + half * 64, 64), 64)
            down_o[rows, :] = piece[0, :64, :].astype(F32)
            held_up[rows, :] = piece[0, 64:128, :].astype(F32)
            held[place, pl.ds(pl.multiple_of(half * 64, 64), 64), :] = piece[0, 128:, :].astype(F32)
    up_o[...] = held_up[...].T
    out_o[...] = held[0]
    for w in range(3):
        qkv_o[w] = held[1 + w].T


def unpack(where, pieces):
    args = [(p, pl.BlockSpec((1, 192, BLK), lambda q, s: (q, 0, 0))) for p in pieces]
    outs = [
        ((2048, BLK), F32, pl.BlockSpec((BLK, BLK), lambda q, s: (q, 0))),
        ((BLK, 2048), F32, pl.BlockSpec((BLK, BLK), lambda q, s: (0, q))),
        ((BLK, BLK), F32, pl.BlockSpec((128, BLK), lambda q, s: (q, 0))),
        ((3, BLK, BLK), F32, pl.BlockSpec((3, BLK, 128), lambda q, s: (0, 0, q))),
    ]
    scratch = [pltpu.VMEM((BLK, BLK), F32), pltpu.VMEM((4, 128, BLK), F32)]
    return call(unpack_kernel, "unpack", 4, where, args, outs, scratch)


def rotation_tables():
    freq = np.power(np.float32(10000.0), np.float32(-2.0 / ROT) * np.arange(ROT // 2, dtype=np.float32))
    angles = (np.arange(SEQ, dtype=np.float32)[:, None] * freq[None, :]).astype(np.float64)
    cosine, sine = np.cos(angles), np.sin(angles)
    nil, rest = np.zeros_like(sine), np.zeros((SEQ, HD - ROT))
    tables = ([cosine, cosine, rest + 1.0], [-sine, nil, rest], [nil, sine, rest])
    return [jnp.asarray(np.concatenate(t * 2, 1).astype(np.float32)) for t in tables]


class Order:
    def __init__(self):
        self.before = []

    def hold(self):
        gate = tuple(self.before)
        return lambda value: after(value, *gate) if gate else value

    def do(self, step):
        self.before = list(step(self.hold()))

    def go(self, step):
        return list(step(self.hold()))

    def wait(self, arrivals):
        self.before = self.before + arrivals


def shards(
    tokens,
    norm_gain,
    norm_bias,
    qkv_weight,
    qkv_bias,
    up_weight,
    up_bias,
    out_weight,
    out_bias,
    down_weight,
    down_bias,
    cotangent,
):
    r = lax.axis_index("row").astype(jnp.int32)
    c = lax.axis_index("col").astype(jnp.int32)
    g = lax.axis_index("dp").astype(jnp.int32)
    x, half = g % 4, g // 4
    r1, x1, c1 = r.reshape(1), x.reshape(1), c.reshape(1)

    raw = (qkv_weight, up_weight, out_weight, down_weight)
    tables = rotation_tables()
    bias = jnp.concatenate([qkv_bias[0], qkv_bias[1], qkv_bias[2], up_bias]).reshape(1, 896)
    have = SimpleNamespace(own=jnp.stack([tokens, cotangent]), middle=None, sums_c=[])

    def send(name, source, move):
        def step(hold):
            setattr(have, name, move(hold(getattr(have, source))))
            return [getattr(have, name)]

        return step

    def twin(name):
        return send(name + "_twin", name, lambda v: from_col(v, 1))

    def over(name):
        return send(name + "_across", name, lambda v: from_col(v, 2))

    def own_rows(hold):
        own = hold(have.own)
        have.nxt, have.prv = from_row(own, 1), from_row(own, 3)
        return [have.nxt, have.prv]

    def far_prep(hold):
        have.packs = prep_far(c, x, hold(raw[0]), *raw[1:])
        return have.packs

    def near_prep(hold):
        have.wf0, have.wb0, have.pack = prep_near(c1, hold(raw[0]), *raw[1:])
        return [have.pack]

    def send_packs(hold):
        have.packs = [from_col(hold(v), k) for v, k in zip(have.packs, (2, 3))]
        return have.packs

    def send_norms(hold):
        norms = jnp.broadcast_to(hold(jnp.stack([norm_gain, norm_bias]))[None], (4, 2, BLK))
        have.norms = lax.all_to_all(norms, "col", 0, 0)
        return [have.norms]

    def send_far(hold):
        have.fars = [from_row(hold(have.nxt[0]), 1), from_row(hold(have.prv[1]), 3)]
        return have.fars

    def stack_far(hold):
        have.far = jnp.stack([hold(have.fars[0]), have.fars[1]])
        return [have.far]

    def stack_packs(hold):
        have.pair = jnp.stack([hold(have.packs[0]), have.packs[1]])
        return [have.pair]

    def send_pair(hold):
        pair = hold(have.pair)
        have.pairs = [from_x(pair, 1), from_x(pair, 3)]
        return have.pairs

    def slice_pairs(hold):
        nxt, prv = have.pairs
        have.pair_far = [hold(nxt[0]), prv[1]]
        return have.pair_far

    def send_pair_far(hold):
        a, b = have.pair_far
        have.pair_far = [from_x(hold(a), 1), from_x(hold(b), 3)]
        return have.pair_far

    def ring(hold):
        v = hold(have.across)
        have.nxt_across, have.prv_across = from_row(v, 1), from_row(v, 3)
        return [have.nxt_across, have.prv_across]

    def twins(names):
        parts = [twin(n) for n in names]
        return lambda hold: [v for p in parts for v in p(hold)]

    def join_packs(hold):
        parts = [hold(have.packs[0]), have.packs[1], *have.pairs, *have.pair_far, have.pack_twin]
        done = join(x1, parts)
        have.wf, have.wb = (have.wf0, *done[:3]), (have.wb0, *done[3:])
        return [done[0]]

    def middle_step(n):
        row = ("own", "nxt", "prv", "far")[n]
        across = ("across", "nxt_across", "prv_across", "far_across")[n]

        def step(hold):
            pieces = [getattr(have, k) for k in (row, row + "_twin", across, across + "_twin")]
            norms = [lax.dynamic_index_in_dim(have.norms, c ^ k, 0, False) for k in range(4)]
            norms = jnp.concatenate(norms, 1)
            shared = (have.wf, have.wb, norms[0:1], norms[1:2], bias, tables)
            done = middle(r1, n, [hold(pieces[0])] + pieces[1:], shared, have.middle)
            if n == 0:
                have.hat, have.inv = done[10:]
            have.middle = done[:8]
            have.sums_c = have.sums_c + [done[8:10]]
            return [done[8]]

        return step

    norm_sum = GroupSum(lambda a, b, w: dot_nt(a[...], w[:, :384]) + dot_nt(b[...], w[:, 384:]), "norm_grad")
    layer_sum = GroupSum(lambda a, b, w: dot_nn(a[...], w[:128]) + dot_nn(b[...], w[128:]), "layer")

    def mlp_weights(hold):
        normed, cot = have.middle[:2]
        lefts = [hold(have.middle[6]), have.middle[7]]
        have.first = WeightSum(weights(mlp_weights_kernel, x1, lefts, cot, normed, 256, "mlp_weights"))
        return have.first.chunks

    def attention_all(hold):
        qkv, att_grad, hidden, up_grad = have.middle[2:6]
        attended, qkv_grad, att_t, qkvg_t, qkv_sum = attention(r1, hold(qkv), att_grad, tables)
        norm_sum.first, norm_sum.second, norm_sum.ws = qkv_grad, up_grad, have.wf
        layer_sum.first, layer_sum.second, layer_sum.ws = attended, hidden, have.wb
        have.__dict__.update(att_t=att_t, qkvg_t=qkvg_t, qkv_sum=qkv_sum)
        return [qkv_sum]

    def att_weights(hold):
        normed, cot = have.middle[:2]
        lefts = [hold(have.att_t), have.qkvg_t]
        have.second = WeightSum(weights(att_weights_kernel, x1, lefts, cot, normed, 128, "att_weights"))
        return have.second.chunks

    def tiles(hold):
        first, second = have.first, have.second
        first.add(hold)
        second.add(hold)
        have.gather = Gather(jnp.concatenate([first.tiles, second.tiles], 1))
        return [have.gather.tiles]

    def normed_total(hold):
        normed_grad = hold(norm_sum.keep) + norm_sum.across.astype(F32)
        hat = have.hat
        up_sum, cot_sum = sum(v[0] for v in have.sums_c), sum(v[1] for v in have.sums_c)
        hat_grad = normed_grad * norm_gain
        have.hat_grad = hat_grad
        have.sums = jnp.stack([jnp.sum(hat_grad, 1), jnp.sum(hat_grad * hat, 1)])
        vectors = [have.qkv_sum, up_sum, cot_sum]
        vectors += [jnp.sum(normed_grad * hat, 0, keepdims=True), jnp.sum(normed_grad, 0, keepdims=True)]
        vectors = jnp.concatenate(vectors, 1).reshape(1, 19, 128)
        have.vectors = jnp.broadcast_to(vectors, (32, 19, 128))
        return [have.sums, have.vectors]

    def send_sums(hold):
        sums = hold(have.sums)
        have.sums_got = [from_col(sums, k) for k in (1, 2, 3)]
        return have.sums_got

    def send_vectors(hold):
        have.vectors = lax.all_to_all(hold(have.vectors), ("dp", "row"), 0, 0, tiled=True)
        return [have.vectors]

    def token_grads(hold):
        sums = (hold(have.sums) + sum(have.sums_got)) / D
        hat_grad, hat, inv = have.hat_grad, have.hat, have.inv
        have.tokens_grad = cotangent.astype(F32) + inv * (
            hat_grad - sums[0][:, None] - hat * sums[1][:, None]
        )
        return [have.tokens_grad]

    def unpack_all(hold):
        pieces = have.gather.pieces()
        have.weight_grads = unpack(jnp.stack([x, half]), [hold(pieces[0])] + pieces[1:])
        return have.weight_grads[2:3]

    def last_sum(hold):
        total = layer_sum.total() + out_bias.astype(F32) + down_bias.astype(F32)
        have.layer_out = (hold(tokens).astype(F32) + total).astype(BF16)
        return [have.layer_out]

    order = Order()
    own_rows_moved = order.go(own_rows)
    across_moved = order.go(send("across", "own", lambda v: from_col(v, 2)))
    order.do(far_prep)
    packs_moved = order.go(send_packs)
    own_twin_moved = order.go(twin("own"))
    norms_moved = order.go(send_norms)
    order.wait(packs_moved)
    order.do(stack_packs)
    pairs_moved = order.go(send_pair)
    order.wait(own_twin_moved)
    order.wait(norms_moved)
    order.wait(own_rows_moved)
    far_moved = order.go(send_far)
    order.do(near_prep)
    order.wait(far_moved)
    order.do(stack_far)
    across_twin_moved = order.go(twin("across"))
    order.wait(across_twin_moved)
    ring_moved = order.go(ring)
    order.go(over("far"))
    order.wait(across_moved)
    order.wait(pairs_moved)
    order.do(slice_pairs)
    order.go(send_pair_far)
    order.go(twin("pack"))
    order.do(join_packs)
    order.do(middle_step(0))
    order.go(twins(("nxt", "prv")))
    order.wait(ring_moved)
    far_twin_moved = order.go(twin("far"))
    ring_twins_moved = order.go(twins(("nxt_across", "prv_across")))
    far_across_twin_moved = order.go(twin("far_across"))
    order.wait(ring_twins_moved)
    order.do(middle_step(1))
    order.wait(far_twin_moved)
    order.do(middle_step(2))
    order.wait(far_across_twin_moved)
    order.do(middle_step(3))
    order.do(mlp_weights)
    first_near_moved = order.go(lambda hold: have.first.send((1, 3), hold))
    order.do(attention_all)
    order.do(norm_sum.odd)
    order.wait(first_near_moved)
    order.go(lambda hold: have.first.send((2,), hold))
    norm_swap_moved = order.go(norm_sum.move_swap)
    order.do(att_weights)
    second_far_moved = order.go(lambda hold: have.second.send((2,), hold))
    order.wait(norm_swap_moved)
    order.do(lambda hold: have.first.split(c1, hold))
    first_exchange_moved = order.go(lambda hold: have.first.exchange(hold))
    second_near_moved = order.go(lambda hold: have.second.send((1, 3), hold))
    order.do(norm_sum.even)
    norm_rows_moved = order.go(norm_sum.move_rows)
    order.do(layer_sum.odd)
    order.wait(first_exchange_moved)
    order.wait(second_far_moved)
    order.do(lambda hold: have.second.split(c1, hold))
    second_exchange_moved = order.go(lambda hold: have.second.exchange(hold))
    layer_swap_moved = order.go(layer_sum.move_swap)
    order.wait(second_near_moved)
    order.wait(second_exchange_moved)
    order.do(tiles)
    gather_half_moved = order.go(lambda hold: have.gather.other_half(hold))
    gather_a_moved = order.go(lambda hold: have.gather.first(hold))
    order.wait(layer_swap_moved)
    order.do(lambda hold: layer_sum.all_rows(r1, hold))
    layer_rows_moved = order.go(layer_sum.exchange_rows)
    order.wait(norm_rows_moved)
    order.do(norm_sum.own)
    norm_across_moved = order.go(norm_sum.move_across)
    order.wait(gather_half_moved)
    order.wait(gather_a_moved)
    gather_b_moved = order.go(lambda hold: have.gather.second(hold))
    order.wait(norm_across_moved)
    order.do(normed_total)
    sums_moved = order.go(send_sums)
    order.wait(sums_moved)
    order.do(token_grads)
    order.wait(gather_b_moved)
    gather_far_moved = order.go(lambda hold: have.gather.third(hold))
    order.wait(layer_rows_moved)
    order.do(layer_sum.sum_rows)
    layer_across_moved = order.go(layer_sum.move_across)
    vectors_moved = order.go(send_vectors)
    order.wait(gather_far_moved)
    order.do(unpack_all)
    order.wait(layer_across_moved)
    order.wait(vectors_moved)
    order.do(last_sum)
    down_grad, up_wgrad, out_grad, qkv_wgrad = have.weight_grads
    layer_out, tokens_grad = have.layer_out, have.tokens_grad
    vectors = have.vectors.reshape(8, 4, 19, 128)
    biases = jnp.sum(lax.dynamic_slice_in_dim(vectors, r, 1, 1)[:, 0, :11], 0).reshape(-1)
    norm_grads = jnp.sum(vectors[:, :, 11:], (0, 1)).reshape(-1)
    return (
        layer_out,
        tokens_grad,
        norm_grads[:BLK],
        norm_grads[BLK:],
        qkv_wgrad,
        biases[:384].reshape(3, 128),
        up_wgrad,
        biases[384:896],
        out_grad,
        biases[896:],
        down_grad,
        biases[896:],
    )


def solution(mesh):
    in_specs = (
        P(("dp", "row"), "col"),
        P("col"),
        P("col"),
        P(None, "col", "row"),
        P(None, ("row", "col")),
        P("col", "row"),
        P(("row", "col")),
        P("row", "col"),
        P("col"),
        P("row", "col"),
        P("col"),
        P(("dp", "row"), "col"),
    )
    out_specs = (
        P(("dp", "row"), "col"),
        P(("dp", "row"), "col"),
        P("col"),
        P("col"),
        P(None, "col", "row"),
        P(None, ("row", "col")),
        P("col", "row"),
        P(("row", "col")),
        P("row", "col"),
        P("col"),
        P("row", "col"),
        P("col"),
    )
    return jax.shard_map(shards, mesh=mesh, in_specs=in_specs, out_specs=out_specs, check_vma=False)
```

```python
import math
from types import SimpleNamespace

import jax
import jax.numpy as jnp
import numpy as np
from jax import lax
from jax.experimental import pallas as pl
from jax.experimental.pallas import tpu as pltpu
from jax.sharding import PartitionSpec as P

D = 2048
HD = 64
ROT = 32
SEQ = 1024
EPS = 1e-05
BLK = 512
F32 = jnp.float32
BF16 = jnp.bfloat16
MIB = 1 << 20
GELU_C = math.sqrt(2.0 / math.pi)


def from_col(value, k):
    return lax.ppermute(value, "col", [(i, i ^ k) for i in range(4)])


def from_row(value, k):
    return lax.ppermute(value, "row", [((i + k) % 4, i) for i in range(4)])


def from_x(value, k):
    return lax.ppermute(value, "dp", [(i // 4 * 4 + (i + k) % 4, i) for i in range(8)])


def from_half(value):
    return lax.ppermute(value, "dp", [(i, (i + 4) % 8) for i in range(8)])


def after(value, *others):
    return lax.optimization_barrier((value, *others))[0]


def dot_nn(a, b):
    return jnp.dot(a, b, preferred_element_type=F32)


def dot_nt(a, b):
    return lax.dot_general(a, b, (((1,), (1,)), ((), ())), preferred_element_type=F32)


def dot_tn(a, b):
    return lax.dot_general(a, b, (((0,), (0,)), ((), ())), preferred_element_type=F32)


def turned(v, cosine, sine_up, sine_down):
    return v * cosine + pltpu.roll(v, 112, 1) * sine_up + pltpu.roll(v, 16, 1) * sine_down


LIMITS = {}


def once(shape):
    return pl.BlockSpec(shape, lambda *_: (0,) * len(shape), pipeline_mode=pl.Buffered(1))


def call(kernel, name, grid, scalars, args, outs, scratch=(), aliases=None):
    return pl.pallas_call(
        kernel,
        grid_spec=pltpu.PrefetchScalarGridSpec(
            num_scalar_prefetch=1,
            grid=(grid,),
            in_specs=[spec for _, spec in args],
            out_specs=[spec for _, _, spec in outs],
            scratch_shapes=list(scratch),
        ),
        out_shape=[jax.ShapeDtypeStruct(shape, dtype) for shape, dtype, _ in outs],
        input_output_aliases=aliases or {},
        compiler_params=pltpu.CompilerParams(vmem_limit_bytes=next((v for k, v in LIMITS.items() if k in name), 52) * MIB),
        cost_estimate=pl.CostEstimate(flops=1000, bytes_accessed=1000, transcendentals=0),
        name=name,
    )(scalars, *[v for v, _ in args])


RESIDENT = pl.BlockSpec(memory_space=pltpu.VMEM)


def full(array):
    return (array, once(array.shape))


def out_full(shape, dtype):
    return (shape, dtype, once(shape))


STEP = 512
PER = BLK // STEP


def packed(far, qkv, up, out, down):
    for w in range(3):
        far[w * 128 : (w + 1) * 128, :] = qkv(w)
    for n in range(4):
        far[384 + n * 128 : 512 + n * 128, :] = up(n)
        far[896 + n * 160 : 928 + n * 160, :] = out(n)
        far[928 + n * 160 : 1056 + n * 160, :] = down(n)


def lanes(t):
    return pl.ds(pl.multiple_of(t * 128, 128), 128)


def prep_near_kernel(s_ref, qkv, up, out, down, front, back, twin):
    c = s_ref[0]
    for w in range(3):
        front[:, w * 128 : (w + 1) * 128] = qkv[w, :, lanes(c)]
    front[:, 384:] = up[:, pl.ds(pl.multiple_of(c * BLK, BLK), BLK)]
    back[0:128, :] = out[lanes(c), :]
    back[128:, :] = down[pl.ds(pl.multiple_of(c * BLK, BLK), BLK), :]
    t = c ^ 1
    for k in range(4):
        feats = slice(k * 128, (k + 1) * 128)
        packed(
            twin.at[k],
            lambda w: qkv[w, feats, lanes(t)],
            lambda n: up[feats, lanes(t * 4 + n)],
            lambda n: out[pl.ds(pl.multiple_of(t * 128 + k * 32, 32), 32), n * 128 : (n + 1) * 128],
            lambda n: down[lanes(t * 4 + k), n * 128 : (n + 1) * 128],
        )


def prep_near(c, *raw):
    outs = [((BLK, 896), BF16, RESIDENT), ((640, BLK), BF16, RESIDENT), out_full((4, 1536, 128), BF16)]
    return call(prep_near_kernel, "prep_near", 1, c, [full(w) for w in raw], outs)


def prep_far_kernel(s_ref, qkv, up, *refs):
    for n, k in enumerate((2, 3)):
        t = s_ref[0] ^ k
        out, down = refs[n], refs[2 + n]
        packed(
            refs[4 + n],
            lambda w: qkv[w, :, lanes(t)],
            lambda n: up[:, lanes(t * 4 + n)],
            lambda n: out[:, n * 128 : (n + 1) * 128],
            lambda n: down[:, n * 128 : (n + 1) * 128],
        )


def prep_far(c, x, qkv_weight, up_weight, out_weight, down_weight):
    args = [
        (qkv_weight, pl.BlockSpec((3, 128, BLK), lambda i, s: (0, s[1], 0))),
        (up_weight, pl.BlockSpec((128, 2048), lambda i, s: (s[1], 0))),
    ]
    args += [(out_weight, pl.BlockSpec((32, BLK), lambda i, s, k=k: ((s[0] ^ k) * 4 + s[1], 0))) for k in (2, 3)]
    args += [(down_weight, pl.BlockSpec((128, BLK), lambda i, s, k=k: ((s[0] ^ k) * 4 + s[1], 0))) for k in (2, 3)]
    return call(prep_far_kernel, "prep_far", 1, jnp.stack([c, x]), args, [out_full((1536, 128), BF16)] * 2)


def unpacked(part, place, wf, wb):
    feats = pl.ds(pl.multiple_of(place * 128, 128), 128)
    for n in range(7):
        wf[feats, n * 128 : (n + 1) * 128] = part[n * 128 : (n + 1) * 128, :]
    rows = pl.ds(pl.multiple_of(place * 32, 32), 32)
    wide = pl.ds(pl.multiple_of(128 + place * 128, 128), 128)
    for n in range(4):
        cols = slice(n * 128, (n + 1) * 128)
        wb[rows, cols] = part[896 + n * 160 : 928 + n * 160, :]
        wb[wide, cols] = part[928 + n * 160 : 1056 + n * 160, :]


def join_kernel(s_ref, own2, own3, nxt, prv, far2, far3, twin, wf1, wf2, wf3, wb1, wb2, wb3):
    x = s_ref[0]
    for k in range(4):
        unpacked(twin.at[k], k, wf1, wb1)
        unpacked((own2, nxt.at[0], far2, prv.at[0])[k], (x + k) % 4, wf2, wb2)
        unpacked((own3, nxt.at[1], far3, prv.at[1])[k], (x + k) % 4, wf3, wb3)


def join(x, parts):
    outs = [((BLK, 896), BF16, RESIDENT)] * 3 + [((640, BLK), BF16, RESIDENT)] * 3
    return call(join_kernel, "join", 1, x, [full(p) for p in parts], outs)


ORDER = (0, 1, 3, 2)
WIDTHS = ((D, BF16), (D, BF16), (384, BF16), (128, BF16), (BLK, BF16), (BLK, BF16))


def middle_kernel(extra, own, r_ref, *refs):
    step = pl.program_id(0)
    ps, rest = refs[:4], refs[4:]
    wf, wb = rest[0:4], rest[4:8]
    gain, shift, bias, cos_t, up_t, down_t = rest[8:14]
    rest = rest[14 + extra :]
    normed_o, cot_o, qkv_o, att_o, hidden_o, up_o, hidden_t, upg_t, up_sum, cot_sum = rest[:10]
    columns = [slice(q * BLK, (q + 1) * BLK) for q in range(4)]

    xs = [p[0].astype(F32) for p in ps]
    center = jnp.sum(xs[0] + xs[1] + xs[2] + xs[3], 1, keepdims=True) * (1.0 / D)
    xs = [x - center for x in xs]
    squares = xs[0] * xs[0] + xs[1] * xs[1] + xs[2] * xs[2] + xs[3] * xs[3]
    inv = lax.rsqrt(jnp.sum(squares, 1, keepdims=True) * (1.0 / D) + EPS)
    for q, cols in enumerate(columns):
        hat = xs[q] * inv
        if own and q == 0:
            rest[10][...] = hat
            rest[11][...] = inv
        normed_o[:, cols] = (hat * gain[:, cols] + shift[:, cols]).astype(BF16)
    acc = bias[...].astype(F32)
    grad = None
    for q, cols in enumerate(columns):
        acc = acc + dot_nn(normed_o[:, cols], wf[q][...])
        block = ps[q][1]
        cot_o[:, cols] = block
        term = dot_nt(block, wb[q][...])
        grad = term if grad is None else grad + term
    cosine, sine_up, sine_down = cos_t[...], up_t[...], down_t[...]
    for k in range(2):
        qkv_o[:, k * 128 : (k + 1) * 128] = turned(
            acc[:, k * 128 : (k + 1) * 128], cosine, sine_up, sine_down
        ).astype(BF16)
    qkv_o[:, 256:384] = acc[:, 256:384].astype(BF16)
    att_o[...] = grad[:, :128].astype(BF16)
    u = acc[:, 384:]
    sq = u * u
    t = jnp.tanh(GELU_C * u * (1.0 + 0.044715 * sq))
    half = 0.5 * (1.0 + t)
    hidden = (u * half).astype(BF16)
    hidden_o[...] = hidden
    hidden_t[...] = hidden.T
    slope = half + (0.5 * GELU_C) * u * (1.0 - t * t) * (1.0 + (3 * 0.044715) * sq)
    up = (grad[:, 128:] * slope).astype(BF16)
    up_o[...] = up
    upg_t[...] = up.T

    @pl.when(step == 0)
    def _():
        up_sum[...] = jnp.zeros_like(up_sum)
        cot_sum[...] = jnp.zeros_like(cot_sum)

    up_sum[...] += jnp.sum(up.astype(F32), 0, keepdims=True)
    cot_sum[...] += jnp.sum(ps[0][1].astype(F32), 0, keepdims=True)


def middle(r, n, pieces, shared, bufs=None):
    wf, wb, gain, shift, bias, tables = shared
    first, odd = n * PER, ORDER[n] % 2
    args = [(v, pl.BlockSpec((2, STEP, BLK), lambda i, r: (0, i, 0))) for v in pieces]
    args += [(v, RESIDENT) for v in (*wf, *wb)] + [full(v) for v in (gain, shift, bias)]
    args += [(t, pl.BlockSpec((STEP, 128), lambda i, r: ((r[0] + odd) % 2 * PER + i, 0))) for t in tables]
    aliases = {}
    if bufs is not None:
        aliases = {1 + len(args) + n: n for n in range(8)}
        args += [(v, pl.BlockSpec(memory_space=pl.ANY)) for v in bufs]
    outs = [((2048, w), t, pl.BlockSpec((STEP, w), lambda i, r: (first + i, 0))) for w, t in WIDTHS]
    outs += [((BLK, 2048), BF16, pl.BlockSpec((BLK, STEP), lambda i, r: (0, first + i)))] * 2
    outs += [out_full((1, BLK), F32)] * 2
    if bufs is None:
        outs += [((BLK, w), F32, pl.BlockSpec((STEP, w), lambda i, r: (i, 0))) for w in (BLK, 1)]

    def kernel(*refs):
        middle_kernel(len(aliases), bufs is None, *refs)

    return call(kernel, "middle", PER, r, args, outs, (), aliases)


QB = 256


def attention_kernel(r_ref, qkv, grad, cos_t, up_t, down_t, att_o, qkvg_o, att_t, qkvg_t, qkv_sum,
                     seq_in, seq_grad, att_s, qkvg_s, dk, dv):
    r = r_ref[0]

    def places():
        for n, j in enumerate(ORDER):
            yield slice(n * BLK, (n + 1) * BLK), pl.ds(pl.multiple_of(((r + j) % 4) * BLK, BLK), BLK)

    for here, spot in places():
        seq_in[spot, :] = qkv[here, :]
        seq_grad[spot, :] = grad[here, :]
    lane = lax.broadcasted_iota(jnp.int32, (1, 128), 1)
    heads = [lane < HD, lane >= HD]
    causal = lax.broadcasted_iota(jnp.int32, (QB, QB), 1) <= lax.broadcasted_iota(jnp.int32, (QB, QB), 0)
    scale = 1.0 / math.sqrt(HD)
    zero = jnp.zeros((), BF16)

    def sequence(s, carry):
        base = pl.multiple_of(s * SEQ, SEQ)
        dk[...] = jnp.zeros_like(dk)
        dv[...] = jnp.zeros_like(dv)
        for i in range(SEQ // QB):
            table = slice(i * QB, (i + 1) * QB)
            rows = pl.ds(pl.multiple_of(base + i * QB, QB), QB)
            length = (i + 1) * QB
            span = pl.ds(base, length)
            out = jnp.zeros((QB, 128), F32)
            dq = jnp.zeros((QB, 128), F32)
            q_all = seq_in[rows, 0:128] * jnp.asarray(scale, BF16)
            g_all = seq_grad[rows, :]
            keys = seq_in[span, 128:256]
            values = seq_in[span, 256:384]
            stacks = ([], [], [], [])
            for head in heads:
                q = jnp.where(head, q_all, zero)
                g = jnp.where(head, g_all, zero)
                scores = dot_nt(q, keys)
                last = jnp.where(causal, scores[:, length - QB :], -1e30)
                scores = last if i == 0 else jnp.concatenate([scores[:, : length - QB], last], 1)
                peak = jnp.max(scores, 1, keepdims=True)
                powers = jnp.exp(scores - peak)
                probs = powers * (1.0 / jnp.sum(powers, 1, keepdims=True))
                pg = dot_nt(g, values)
                prod = probs * pg
                score_grad = (prod - probs * jnp.sum(prod, 1, keepdims=True)).astype(BF16)
                low = probs.astype(BF16)
                out = out + dot_nn(low, jnp.where(head, values, zero))
                dq = dq + dot_nn(score_grad, jnp.where(head, keys, zero))
                for stack, value in zip(stacks, (score_grad, q, low, g)):
                    stack.append(value)
            score_grads, qs, lows, gs = [jnp.concatenate(stack, 0) for stack in stacks]
            dk[:length, :] += dot_nn(score_grads.T, qs)
            dv[:length, :] += dot_nn(lows.T, gs)
            att_s[rows, :] = out.astype(BF16)
            qkvg_s[rows, 0:128] = turned(
                dq * scale, cos_t[table, :], -up_t[table, :], -down_t[table, :]
            ).astype(BF16)
        whole = pl.ds(base, SEQ)
        qkvg_s[whole, 128:256] = turned(dk[...], cos_t[...], -up_t[...], -down_t[...]).astype(BF16)
        qkvg_s[whole, 256:384] = dv[...].astype(BF16)
        return carry

    lax.fori_loop(0, 2, sequence, 0)
    total = jnp.zeros((1, 384), F32)
    for here, spot in places():
        att, qkvg = att_s[spot, :], qkvg_s[spot, :]
        att_o[here, :] = att
        qkvg_o[here, :] = qkvg
        att_t[:, here] = att.T
        qkvg_t[:, here] = qkvg.T
        total = total + jnp.sum(qkvg.astype(F32), 0, keepdims=True)
    qkv_sum[...] = total


def attention(r, qkv, grad, tables):
    shapes = [((2048, 128), BF16), ((2048, 384), BF16), ((128, 2048), BF16), ((384, 2048), BF16), ((1, 384), F32)]
    scratch = [
        pltpu.VMEM((2048, 384), BF16),
        pltpu.VMEM((2048, 128), BF16),
        pltpu.VMEM((2048, 128), BF16),
        pltpu.VMEM((2048, 384), BF16),
        pltpu.VMEM((SEQ, 128), F32),
        pltpu.VMEM((SEQ, 128), F32),
    ]
    args = [full(v) for v in (qkv, grad, *tables)]
    return call(attention_kernel, "attention", 1, r, args, [out_full(*v) for v in shapes], scratch)


def chunks_out(x, held, outs):
    for k in range(4):
        outs[k][...] = held[(x + k) % 4]


def mlp_weights_kernel(x_ref, hidden_t, upg_t, cot, normed, *refs):
    outs, held = refs[:4], refs[4]
    down = dot_nn(hidden_t[...], cot[...])
    up = dot_nn(upg_t[...], normed[...])
    for a in range(4):
        for h in range(2):
            rows = slice(a * 128 + h * 64, a * 128 + h * 64 + 64)
            held[a, h * 128 : h * 128 + 64, :] = down[rows].astype(BF16)
            held[a, h * 128 + 64 : h * 128 + 128, :] = up[rows].astype(BF16)
    chunks_out(x_ref[0], held, outs)


def att_weights_kernel(x_ref, att_t, qkvg_t, cot, normed, *refs):
    outs, held = refs[:4], refs[4]
    held[0] = dot_nn(att_t[...], cot[...]).astype(BF16)
    qkv = dot_nn(qkvg_t[...], normed[...])
    for w in range(3):
        held[1 + w] = qkv[w * 128 : (w + 1) * 128].astype(BF16)
    chunks_out(x_ref[0], held, outs)


def weights(kernel, x, lefts, cot, normed, rows, name):
    column = lambda q, s: (0, q)
    args = [full(v) for v in lefts] + [(v, pl.BlockSpec((2048, BLK), column)) for v in (cot, normed)]
    outs = [((rows, D), BF16, pl.BlockSpec((rows, BLK), column))] * 4
    return call(kernel, name, 4, x, args, outs, [pltpu.VMEM((4, rows, BLK), BF16)])


def rows_of(width, first):
    return pl.BlockSpec((BLK, width), lambda i, s: (first + i, 0))


class GroupSum:
    def __init__(self, product, name):
        self.product, self.name = product, name

    def run(self, kernel, name, start, blocks, ws, args, outs, hold, scalars=None):
        first, second = hold(self.first), self.second
        pair = [(first, rows_of(first.shape[1], start)), (second, rows_of(second.shape[1], start))]
        if scalars is None:
            scalars = jnp.zeros((1,), jnp.int32)
        ws = [(self.ws[q], RESIDENT) for q in ws]
        return call(kernel, self.name + name, blocks, scalars, pair + ws + args, outs)

    def odd(self, hold):
        def kernel(_, a, b, w1, w3, out):
            for n, w in enumerate((w1, w3)):
                out[:, n * BLK : (n + 1) * BLK] = self.product(a, b, w).astype(BF16)

        outs = [((2048, 2 * BLK), BF16, rows_of(2 * BLK, 0))]
        self.odds = self.run(kernel, "_odd", 0, 4, (1, 3), [], outs, hold)[0]
        return [self.odds]

    def even(self, hold):
        def kernel(_, a, b, w0, w2, odds, *outs):
            totals = [self.product(a, b, w) for w in (w0, w2)]
            total = (jnp.concatenate(totals, 1) + odds[...].astype(F32)).astype(BF16)
            for k in range(3):

                @pl.when(pl.program_id(0) == k)
                def _():
                    outs[k][...] = total

        args = [(self.odds, rows_of(2 * BLK, 1))]
        outs = [out_full((BLK, 2 * BLK), BF16)] * 3
        self.parts = self.run(kernel, "_even", 1, 3, (0, 2), args, outs, hold)
        return self.parts

    def all_rows(self, r, hold):
        def kernel(_, a, b, w0, w2, odds, out):
            totals = [self.product(a, b, w) for w in (w0, w2)]
            out[0] = (jnp.concatenate(totals, 1) + odds[...].astype(F32)).astype(BF16)

        def place(i, s):
            return ((s[0] + jnp.where(i < 2, i, 5 - i)) % 4, 0, 0)

        args = [(self.odds, rows_of(2 * BLK, 0))]
        outs = [((4, BLK, 2 * BLK), BF16, pl.BlockSpec((1, BLK, 2 * BLK), place))]
        self.parts = self.run(kernel, "_rows", 0, 4, (0, 2), args, outs, hold, r)[0]
        return [self.parts]

    def own(self, hold):
        def kernel(_, a, b, w0, w2, odds, one, two, three, *outs):
            for n, w in enumerate((w0, w2)):
                cols = slice(n * BLK, (n + 1) * BLK)
                total = self.product(a, b, w)
                for v in (odds, one, two, three):
                    total = total + v[:, cols].astype(F32)
                outs[n][...] = total.astype(outs[n].dtype)

        args = [(v, rows_of(2 * BLK, 0)) for v in (self.odds, *self.got)]
        outs = [out_full((BLK, BLK), t) for t in (F32, BF16)]
        self.keep, self.give = self.run(kernel, "_own", 0, 1, (0, 2), args, outs, hold)
        return [self.give]

    def sum_rows(self, hold):
        got = hold(self.got)
        total = sum(got[k].astype(F32) for k in range(4))
        self.keep, self.give = total[:, :BLK], total[:, BLK:].astype(BF16)
        return [self.give]

    def move_swap(self, hold):
        self.odds = from_col(hold(self.odds), 1)
        return [self.odds]

    def move_rows(self, hold):
        self.got = [from_row(hold(v), k) for v, k in zip(self.parts, (3, 1, 2))]
        return self.got

    def exchange_rows(self, hold):
        self.got = lax.all_to_all(hold(self.parts), "row", 0, 0, tiled=True)
        return [self.got]

    def move_across(self, hold):
        self.across = from_col(hold(self.give), 2)
        return [self.across]

    def total(self):
        return self.keep + self.across.astype(F32)


def split_kernel(c_ref, *refs):
    parts, out = refs[:4], refs[4]
    rows = out.shape[1]
    for q in range(4):
        cols = slice(q * BLK, (q + 1) * BLK)
        total = sum(p[:, cols].astype(F32) for p in parts)
        for h in range(2):
            out[h * 4 + (c_ref[0] ^ q)] = total[h * rows : (h + 1) * rows].astype(BF16)


class WeightSum:
    def __init__(self, chunks):
        self.chunks = list(chunks)

    def send(self, steps, hold):
        for k in steps:
            self.chunks[k] = from_x(hold(self.chunks[k]), 4 - k)
        return [self.chunks[k] for k in steps]

    def split(self, c, hold):
        rows = self.chunks[0].shape[0] // 2
        args = [full(v) for v in (hold(self.chunks[0]), *self.chunks[1:])]
        self.parts = call(split_kernel, "split", 1, c, args, [out_full((8, rows, BLK), BF16)])[0]
        return [self.parts]

    def exchange(self, hold):
        groups = [[(h * 4 + x) * 4 + k for h in range(2) for k in range(4)] for x in range(4)]
        self.got = lax.all_to_all(hold(self.parts), ("dp", "col"), 0, 0, tiled=True, axis_index_groups=groups)
        return [self.got]

    def add(self, hold):
        got = hold(self.got)
        self.tiles = (got[:4].astype(F32) + got[4:].astype(F32)).astype(BF16)


class Gather:
    def __init__(self, tiles):
        self.tiles = tiles

    def first(self, hold):
        t = hold(self.tiles)
        self.a = [self.tiles, from_x(t, 1), None, from_x(t, 3)]
        return [self.a[1], self.a[3]]

    def other_half(self, hold):
        self.other = from_half(hold(self.tiles))
        return [self.other]

    def second(self, hold):
        t = hold(self.other)
        self.b = [self.other, from_x(t, 1), None, from_x(t, 3)]
        return [self.b[1], self.b[3]]

    def third(self, hold):
        self.a[2], self.b[2] = from_x(hold(self.a[1]), 1), from_x(hold(self.b[3]), 3)
        return [self.a[2], self.b[2]]

    def pieces(self):
        return [p for pair in zip(self.a, self.b) for p in pair]


def unpack_kernel(s_ref, *refs):
    pieces, down_o, up_o, out_o, qkv_o, held_up, held = refs[:8], *refs[8:]
    for k in range(4):
        for e in range(2):
            piece = pieces[2 * k + e]
            place, half = (s_ref[0] + k) % 4, s_ref[1] ^ e
            rows = pl.ds(pl.multiple_of(place * 128 + half * 64, 64), 64)
            down_o[rows, :] = piece[0, :64, :].astype(F32)
            held_up[rows, :] = piece[0, 64:128, :].astype(F32)
            held[place, pl.ds(pl.multiple_of(half * 64, 64), 64), :] = piece[0, 128:, :].astype(F32)
    up_o[...] = held_up[...].T
    out_o[...] = held[0]
    for w in range(3):
        qkv_o[w] = held[1 + w].T


def unpack(where, pieces):
    args = [(p, pl.BlockSpec((1, 192, BLK), lambda q, s: (q, 0, 0))) for p in pieces]
    outs = [
        ((2048, BLK), F32, pl.BlockSpec((BLK, BLK), lambda q, s: (q, 0))),
        ((BLK, 2048), F32, pl.BlockSpec((BLK, BLK), lambda q, s: (0, q))),
        ((BLK, BLK), F32, pl.BlockSpec((128, BLK), lambda q, s: (q, 0))),
        ((3, BLK, BLK), F32, pl.BlockSpec((3, BLK, 128), lambda q, s: (0, 0, q))),
    ]
    scratch = [pltpu.VMEM((BLK, BLK), F32), pltpu.VMEM((4, 128, BLK), F32)]
    return call(unpack_kernel, "unpack", 4, where, args, outs, scratch)


def rotation_tables():
    freq = np.power(np.float32(10000.0), np.float32(-2.0 / ROT) * np.arange(ROT // 2, dtype=np.float32))
    angles = (np.arange(SEQ, dtype=np.float32)[:, None] * freq[None, :]).astype(np.float64)
    cosine, sine = np.cos(angles), np.sin(angles)
    nil, rest = np.zeros_like(sine), np.zeros((SEQ, HD - ROT))
    tables = ([cosine, cosine, rest + 1.0], [-sine, nil, rest], [nil, sine, rest])
    return [jnp.asarray(np.concatenate(t * 2, 1).astype(np.float32)) for t in tables]


class Order:
    def __init__(self):
        self.before = []

    def hold(self):
        gate = tuple(self.before)
        return lambda value: after(value, *gate) if gate else value

    def do(self, step):
        self.before = list(step(self.hold()))

    def go(self, step):
        return list(step(self.hold()))

    def wait(self, arrivals):
        self.before = self.before + arrivals


def shards(
    tokens,
    norm_gain,
    norm_bias,
    qkv_weight,
    qkv_bias,
    up_weight,
    up_bias,
    out_weight,
    out_bias,
    down_weight,
    down_bias,
    cotangent,
):
    r = lax.axis_index("row").astype(jnp.int32)
    c = lax.axis_index("col").astype(jnp.int32)
    g = lax.axis_index("dp").astype(jnp.int32)
    x, half = g % 4, g // 4
    r1, x1, c1 = r.reshape(1), x.reshape(1), c.reshape(1)

    raw = (qkv_weight, up_weight, out_weight, down_weight)
    tables = rotation_tables()
    bias = jnp.concatenate([qkv_bias[0], qkv_bias[1], qkv_bias[2], up_bias]).reshape(1, 896)
    have = SimpleNamespace(own=jnp.stack([tokens, cotangent]), middle=None, sums_c=[])

    def send(name, source, move):
        def step(hold):
            setattr(have, name, move(hold(getattr(have, source))))
            return [getattr(have, name)]

        return step

    def twin(name):
        return send(name + "_twin", name, lambda v: from_col(v, 1))

    def over(name):
        return send(name + "_across", name, lambda v: from_col(v, 2))

    def own_rows(hold):
        own = hold(have.own)
        have.nxt, have.prv = from_row(own, 1), from_row(own, 3)
        return [have.nxt, have.prv]

    def far_prep(hold):
        have.packs = prep_far(c, x, hold(raw[0]), *raw[1:])
        return have.packs

    def near_prep(hold):
        have.wf0, have.wb0, have.pack = prep_near(c1, hold(raw[0]), *raw[1:])
        return [have.pack]

    def send_packs(hold):
        have.packs = [from_col(hold(v), k) for v, k in zip(have.packs, (2, 3))]
        return have.packs

    def send_norms(hold):
        norms = jnp.broadcast_to(hold(jnp.stack([norm_gain, norm_bias]))[None], (4, 2, BLK))
        have.norms = lax.all_to_all(norms, "col", 0, 0)
        return [have.norms]

    def send_far(hold):
        have.fars = [from_row(hold(have.nxt[0]), 1), from_row(hold(have.prv[1]), 3)]
        return have.fars

    def stack_far(hold):
        have.far = jnp.stack([hold(have.fars[0]), have.fars[1]])
        return [have.far]

    def stack_packs(hold):
        have.pair = jnp.stack([hold(have.packs[0]), have.packs[1]])
        return [have.pair]

    def send_pair(hold):
        pair = hold(have.pair)
        have.pairs = [from_x(pair, 1), from_x(pair, 3)]
        return have.pairs

    def slice_pairs(hold):
        nxt, prv = have.pairs
        have.pair_far = [hold(nxt[0]), prv[1]]
        return have.pair_far

    def send_pair_far(hold):
        a, b = have.pair_far
        have.pair_far = [from_x(hold(a), 1), from_x(hold(b), 3)]
        return have.pair_far

    def ring(hold):
        v = hold(have.across)
        have.nxt_across, have.prv_across = from_row(v, 1), from_row(v, 3)
        return [have.nxt_across, have.prv_across]

    def twins(names):
        parts = [twin(n) for n in names]
        return lambda hold: [v for p in parts for v in p(hold)]

    def join_packs(hold):
        parts = [hold(have.packs[0]), have.packs[1], *have.pairs, *have.pair_far, have.pack_twin]
        done = join(x1, parts)
        have.wf, have.wb = (have.wf0, *done[:3]), (have.wb0, *done[3:])
        return [done[0]]

    def middle_step(n):
        row = ("own", "nxt", "prv", "far")[n]
        across = ("across", "nxt_across", "prv_across", "far_across")[n]

        def step(hold):
            pieces = [getattr(have, k) for k in (row, row + "_twin", across, across + "_twin")]
            norms = [lax.dynamic_index_in_dim(have.norms, c ^ k, 0, False) for k in range(4)]
            norms = jnp.concatenate(norms, 1)
            shared = (have.wf, have.wb, norms[0:1], norms[1:2], bias, tables)
            done = middle(r1, n, [hold(pieces[0])] + pieces[1:], shared, have.middle)
            if n == 0:
                have.hat, have.inv = done[10:]
            have.middle = done[:8]
            have.sums_c = have.sums_c + [done[8:10]]
            return [done[8]]

        return step

    norm_sum = GroupSum(lambda a, b, w: dot_nt(a[...], w[:, :384]) + dot_nt(b[...], w[:, 384:]), "norm_grad")
    layer_sum = GroupSum(lambda a, b, w: dot_nn(a[...], w[:128]) + dot_nn(b[...], w[128:]), "layer")

    def mlp_weights(hold):
        normed, cot = have.middle[:2]
        lefts = [hold(have.middle[6]), have.middle[7]]
        have.first = WeightSum(weights(mlp_weights_kernel, x1, lefts, cot, normed, 256, "mlp_weights"))
        return have.first.chunks

    def attention_all(hold):
        qkv, att_grad, hidden, up_grad = have.middle[2:6]
        attended, qkv_grad, att_t, qkvg_t, qkv_sum = attention(r1, hold(qkv), att_grad, tables)
        norm_sum.first, norm_sum.second, norm_sum.ws = qkv_grad, up_grad, have.wf
        layer_sum.first, layer_sum.second, layer_sum.ws = attended, hidden, have.wb
        have.__dict__.update(att_t=att_t, qkvg_t=qkvg_t, qkv_sum=qkv_sum)
        return [qkv_sum]

    def att_weights(hold):
        normed, cot = have.middle[:2]
        lefts = [hold(have.att_t), have.qkvg_t]
        have.second = WeightSum(weights(att_weights_kernel, x1, lefts, cot, normed, 128, "att_weights"))
        return have.second.chunks

    def tiles(hold):
        first, second = have.first, have.second
        first.add(hold)
        second.add(hold)
        have.gather = Gather(jnp.concatenate([first.tiles, second.tiles], 1))
        return [have.gather.tiles]

    def normed_total(hold):
        normed_grad = hold(norm_sum.keep) + norm_sum.across.astype(F32)
        hat = have.hat
        up_sum, cot_sum = sum(v[0] for v in have.sums_c), sum(v[1] for v in have.sums_c)
        hat_grad = normed_grad * norm_gain
        have.hat_grad = hat_grad
        have.sums = jnp.stack([jnp.sum(hat_grad, 1), jnp.sum(hat_grad * hat, 1)])
        vectors = [have.qkv_sum, up_sum, cot_sum]
        vectors += [jnp.sum(normed_grad * hat, 0, keepdims=True), jnp.sum(normed_grad, 0, keepdims=True)]
        vectors = jnp.concatenate(vectors, 1).reshape(1, 19, 128)
        have.vectors = jnp.broadcast_to(vectors, (32, 19, 128))
        return [have.sums, have.vectors]

    def send_sums(hold):
        sums = hold(have.sums)
        have.sums_got = [from_col(sums, k) for k in (1, 2, 3)]
        return have.sums_got

    def send_vectors(hold):
        have.vectors = lax.all_to_all(hold(have.vectors), ("dp", "row"), 0, 0, tiled=True)
        return [have.vectors]

    def token_grads(hold):
        sums = (hold(have.sums) + sum(have.sums_got)) / D
        hat_grad, hat, inv = have.hat_grad, have.hat, have.inv
        have.tokens_grad = cotangent.astype(F32) + inv * (
            hat_grad - sums[0][:, None] - hat * sums[1][:, None]
        )
        return [have.tokens_grad]

    def unpack_all(hold):
        pieces = have.gather.pieces()
        have.weight_grads = unpack(jnp.stack([x, half]), [hold(pieces[0])] + pieces[1:])
        return have.weight_grads[2:3]

    def last_sum(hold):
        total = layer_sum.total() + out_bias.astype(F32) + down_bias.astype(F32)
        have.layer_out = (hold(tokens).astype(F32) + total).astype(BF16)
        return [have.layer_out]

    order = Order()
    own_rows_moved = order.go(own_rows)
    across_moved = order.go(send("across", "own", lambda v: from_col(v, 2)))
    order.do(far_prep)
    packs_moved = order.go(send_packs)
    own_twin_moved = order.go(twin("own"))
    norms_moved = order.go(send_norms)
    order.wait(packs_moved)
    order.do(stack_packs)
    pairs_moved = order.go(send_pair)
    order.wait(own_twin_moved)
    order.wait(norms_moved)
    order.wait(own_rows_moved)
    far_moved = order.go(send_far)
    order.do(near_prep)
    order.wait(far_moved)
    order.do(stack_far)
    across_twin_moved = order.go(twin("across"))
    order.wait(across_twin_moved)
    ring_moved = order.go(ring)
    order.go(over("far"))
    order.wait(across_moved)
    order.wait(pairs_moved)
    order.do(slice_pairs)
    order.go(send_pair_far)
    order.go(twin("pack"))
    order.do(join_packs)
    order.do(middle_step(0))
    order.go(twins(("nxt", "prv")))
    order.wait(ring_moved)
    far_twin_moved = order.go(twin("far"))
    ring_twins_moved = order.go(twins(("nxt_across", "prv_across")))
    far_across_twin_moved = order.go(twin("far_across"))
    order.wait(ring_twins_moved)
    order.do(middle_step(1))
    order.wait(far_twin_moved)
    order.do(middle_step(2))
    order.wait(far_across_twin_moved)
    order.do(middle_step(3))
    order.do(mlp_weights)
    first_near_moved = order.go(lambda hold: have.first.send((1, 3), hold))
    order.do(attention_all)
    order.do(norm_sum.odd)
    order.wait(first_near_moved)
    order.go(lambda hold: have.first.send((2,), hold))
    norm_swap_moved = order.go(norm_sum.move_swap)
    order.do(att_weights)
    second_far_moved = order.go(lambda hold: have.second.send((2,), hold))
    order.wait(norm_swap_moved)
    order.do(lambda hold: have.first.split(c1, hold))
    first_exchange_moved = order.go(lambda hold: have.first.exchange(hold))
    second_near_moved = order.go(lambda hold: have.second.send((1, 3), hold))
    order.do(norm_sum.even)
    norm_rows_moved = order.go(norm_sum.move_rows)
    order.do(layer_sum.odd)
    order.wait(first_exchange_moved)
    order.wait(second_far_moved)
    order.do(lambda hold: have.second.split(c1, hold))
    second_exchange_moved = order.go(lambda hold: have.second.exchange(hold))
    layer_swap_moved = order.go(layer_sum.move_swap)
    order.wait(second_near_moved)
    order.wait(second_exchange_moved)
    order.do(tiles)
    gather_half_moved = order.go(lambda hold: have.gather.other_half(hold))
    gather_a_moved = order.go(lambda hold: have.gather.first(hold))
    order.wait(layer_swap_moved)
    order.do(lambda hold: layer_sum.all_rows(r1, hold))
    layer_rows_moved = order.go(layer_sum.exchange_rows)
    order.wait(norm_rows_moved)
    order.do(norm_sum.own)
    norm_across_moved = order.go(norm_sum.move_across)
    order.wait(gather_half_moved)
    order.wait(gather_a_moved)
    gather_b_moved = order.go(lambda hold: have.gather.second(hold))
    order.wait(norm_across_moved)
    order.do(normed_total)
    sums_moved = order.go(send_sums)
    order.wait(sums_moved)
    order.do(token_grads)
    order.wait(gather_b_moved)
    gather_far_moved = order.go(lambda hold: have.gather.third(hold))
    order.wait(layer_rows_moved)
    order.do(layer_sum.sum_rows)
    layer_across_moved = order.go(layer_sum.move_across)
    vectors_moved = order.go(send_vectors)
    order.wait(gather_far_moved)
    order.do(unpack_all)
    order.wait(layer_across_moved)
    order.wait(vectors_moved)
    order.do(last_sum)
    down_grad, up_wgrad, out_grad, qkv_wgrad = have.weight_grads
    layer_out, tokens_grad = have.layer_out, have.tokens_grad
    vectors = have.vectors.reshape(8, 4, 19, 128)
    biases = jnp.sum(lax.dynamic_slice_in_dim(vectors, r, 1, 1)[:, 0, :11], 0).reshape(-1)
    norm_grads = jnp.sum(vectors[:, :, 11:], (0, 1)).reshape(-1)
    return (
        layer_out,
        tokens_grad,
        norm_grads[:BLK],
        norm_grads[BLK:],
        qkv_wgrad,
        biases[:384].reshape(3, 128),
        up_wgrad,
        biases[384:896],
        out_grad,
        biases[896:],
        down_grad,
        biases[896:],
    )


def solution(mesh):
    in_specs = (
        P(("dp", "row"), "col"),
        P("col"),
        P("col"),
        P(None, "col", "row"),
        P(None, ("row", "col")),
        P("col", "row"),
        P(("row", "col")),
        P("row", "col"),
        P("col"),
        P("row", "col"),
        P("col"),
        P(("dp", "row"), "col"),
    )
    out_specs = (
        P(("dp", "row"), "col"),
        P(("dp", "row"), "col"),
        P("col"),
        P("col"),
        P(None, "col", "row"),
        P(None, ("row", "col")),
        P("col", "row"),
        P(("row", "col")),
        P("row", "col"),
        P("col"),
        P("row", "col"),
        P("col"),
    )
    return jax.shard_map(shards, mesh=mesh, in_specs=in_specs, out_specs=out_specs, check_vma=False)
```
